256 devices in a mesh: head: 16 (over z, x_lo), ctx: 16 (over y, x_hi, core).
Axes of the slice: x: 4 (x_hi: 2, x_lo: 2; x = x_hi * 2 + x_lo), y: 4, z: 8, core: 2. Of those that a mesh axis runs over, the one named last changes fastest.
Arguments:
- query_latent: bfloat16 [1024, 1536], P('ctx'), may hold values from -6 to 6
- w_query_nope: bfloat16 [1536, 16384], P(None, 'head'), may hold values from -0.15625 to 0.15625
- w_query_rope: bfloat16 [1536, 8192], P(None, 'head'), may hold values from -0.15625 to 0.15625
- w_absorb_key: bfloat16 [128, 128, 512], P('head'), may hold values from -0.5 to 0.5
- w_absorb_value: bfloat16 [128, 512, 128], P('head'), may hold values from -0.25 to 0.25
- w_output: bfloat16 [16384, 7168], P('head', 'ctx'), may hold values from -0.046875 to 0.046875
- latent_cache: bfloat16 [32, 1024, 576], P(None, 'ctx'), may hold values from -250 to 250
- block_lists: int32 [64, 48], replicated, may hold values from 0 to 511, as said below
- block_counts: int32 [64], replicated, may hold values from 24 to 48, as said below
- positions: int32 [1024], replicated, may hold values from 1024 to 8191
Outputs:
- attended: bfloat16 [1024, 7168], P('head', 'ctx')
The draws below stay inside these ranges and needn't reach their ends.
Inputs may be any that keep to these rules, and one draw needn't show every extreme that they name: `block_lists`: entries at or beyond a tile's count are block ids to be ignored. Among a tile's valid entries no block repeats and at most 4 lie in one shard (blocks of equal residue modulo 512 / 32); tile 0 has 4 valid entries in one shard. `block_counts`: tile 0 has 48 valid entries.
All inputs are finite; a program needn't handle non-finite values.
Results may differ from the reference program's by a relative error of at most 0.011.
Values may be sent and summed in bfloat16 or wider, within the bound.
A program may use at most 192 MiB of HBM per device.

```python
import jax
import jax.numpy as jnp
from jax import lax

D = 7168
QL = 1536
LAT = 512
ROPE = 64
NOPE = 128
VDIM = 128
BLK = 64
TILE = 16
MAXB = 48
BLK_DEV = 32
LMAX = 4
HEADS = 128
TOKENS = 1024
TILES = 64
NBLK = 512
N_CTX = 16


def draw_block_lists(key, part):
    key = jax.random.fold_in(key, 11)
    key_one, key_two = jax.random.split(key)
    shard_total = NBLK // BLK_DEV

    def shuffled(subkey):
        return jax.random.permutation(subkey, shard_total)
    shard_order = jax.vmap(shuffled)(jax.random.split(key_one, TILES))
    starts = jax.random.randint(key_two, (TILES, shard_total), 0, BLK_DEV)
    slots = jnp.arange(MAXB)
    later = jnp.maximum(slots - LMAX, 0)
    run_of = jnp.where(slots < LMAX, 0, 1 + later % (shard_total - 1))
    rank_of = jnp.where(slots < LMAX, slots, later // (shard_total - 1))
    shard_of = shard_order[:, run_of]
    start_of = jnp.take_along_axis(starts, shard_of, axis=1)
    local_block = (start_of + rank_of[None, :]) % BLK_DEV
    return (local_block * shard_total + shard_of).astype(jnp.int32)


def draw_block_counts(key, part):
    key = jax.random.fold_in(key, 12)
    counts_drawn = jax.random.randint(key, (TILES,), MAXB // 2, MAXB + 1)
    return counts_drawn.at[0].set(MAXB).astype(jnp.int32)


def draw_latent_cache(key, part):
    key = jax.random.fold_in(key, 13)
    key_one = jax.random.fold_in(key, 0)
    shard_total = NBLK // BLK_DEV
    entries = jnp.clip(jax.random.normal(key_one, (NBLK * BLK, LAT + ROPE), jnp.float32), -4.0, 4.0)
    return entries.reshape(BLK_DEV, shard_total * BLK, LAT + ROPE).astype(jnp.bfloat16)


def plant(drawn, key, low, high):
    place = [jax.random.randint(jax.random.fold_in(key, axis), (), 0, length) for axis, length in enumerate(drawn.shape)]
    main_axis = drawn.shape.index(max(drawn.shape))
    neighbour = place[:main_axis] + [(place[main_axis] + 1) % drawn.shape[main_axis]] + place[main_axis + 1:]
    return drawn.at[tuple(place)].set(low).at[tuple(neighbour)].set(high)


def level_of(key, extent, cuts, least, top_value):
    def one(position, shards_of):
        draws = jax.random.uniform(jax.random.fold_in(jax.random.fold_in(key, 6), position), (shards_of,), jnp.float32, least / len(cuts), top_value / len(cuts))
        return jnp.repeat(jnp.exp(draws), extent[position] // shards_of).reshape((-1,) + (1,) * (len(extent) - position - 1))

    loudness = one(*cuts[0])
    for cut in cuts[1:]:
        loudness = loudness * one(*cut)
    return loudness


def scatter_about(key, extent, scale, bound, cuts=(), held_as=jnp.bfloat16):
    loudness = level_of(key, extent, cuts, -0.22, 0.18) if cuts else 1.0
    values = jax.random.normal(key, extent, jnp.float32) * scale * loudness
    return jnp.minimum(jnp.maximum(values, -bound), bound).astype(held_as)


def setup_inputs(seed: int = 0) -> dict:
    arg_keys = jax.random.split(jax.random.key(seed), 11)
    query_latent = scatter_about(arg_keys[0], (TOKENS, QL), 1.0, 6.0, ((0, 16),))
    w_query_nope = scatter_about(arg_keys[1], (QL, HEADS * NOPE), QL ** -0.5, 0.15625, ((1, 16),))
    w_query_rope = scatter_about(arg_keys[2], (QL, HEADS * ROPE), QL ** -0.5, 0.15625, ((1, 16),))
    w_absorb_key = scatter_about(arg_keys[3], (HEADS, NOPE, LAT), NOPE ** -0.5, 0.5, ((0, 16),))
    w_absorb_value = scatter_about(arg_keys[4], (HEADS, LAT, VDIM), LAT ** -0.5, 0.25, ((0, 16),))
    w_output = scatter_about(arg_keys[5], (HEADS * VDIM, D), (HEADS * VDIM) ** -0.5, 0.046875, ((0, 16), (1, 16)))
    latent_cache = draw_latent_cache(jax.random.fold_in(arg_keys[10], 71), 0)
    block_lists = draw_block_lists(jax.random.fold_in(arg_keys[10], 71), 0)
    block_counts = draw_block_counts(jax.random.fold_in(arg_keys[10], 71), 0)
    positions = plant(jax.random.randint(arg_keys[9], (TOKENS,), 1024, 8192), jax.random.fold_in(arg_keys[9], 1), 1024, 8191).astype(jnp.int32)
    return {"query_latent": query_latent, "w_query_nope": w_query_nope, "w_query_rope": w_query_rope, "w_absorb_key": w_absorb_key, "w_absorb_value": w_absorb_value, "w_output": w_output, "latent_cache": latent_cache, "block_lists": block_lists, "block_counts": block_counts, "positions": positions}


def rotate(rope_part, token_positions):
    half_width = ROPE // 2
    frequency = 10000.0 ** (-2.0 * jnp.arange(half_width).astype(jnp.float32) / ROPE)
    angles = token_positions.astype(jnp.float32)[:, None] * frequency[None, :]
    cosine = jnp.cos(angles)[:, None, :]
    sine_part = jnp.sin(angles)[:, None, :]
    first_half = rope_part[..., :half_width]
    second_half = rope_part[..., half_width:]
    return jnp.concatenate([first_half * cosine - second_half * sine_part, first_half * sine_part + second_half * cosine], axis=-1)


def make_queries(query_latent, w_query_nope, w_query_rope, w_absorb_key, token_positions):
    row_count = query_latent.shape[0]
    head_count = w_absorb_key.shape[0]
    nope_part = jnp.dot(query_latent, w_query_nope, preferred_element_type=jnp.float32).astype(jnp.bfloat16)
    nope_part = nope_part.reshape(row_count, head_count, NOPE)
    latent_part = jnp.einsum("thn,hnl->thl", nope_part.astype(jnp.float32), w_absorb_key.astype(jnp.float32)).astype(jnp.bfloat16)
    rope_part = jnp.dot(query_latent, w_query_rope, preferred_element_type=jnp.float32).reshape(row_count, head_count, ROPE)
    rope_part = rotate(rope_part, token_positions).astype(jnp.bfloat16)
    return jnp.concatenate([latent_part, rope_part], axis=-1)


def reference(query_latent, w_query_nope, w_query_rope, w_absorb_key, w_absorb_value, w_output, latent_cache, block_lists, block_counts, positions):
    queries = make_queries(query_latent, w_query_nope, w_query_rope, w_absorb_key, positions)
    head_count = w_absorb_key.shape[0]
    cache_blocks = latent_cache.reshape(NBLK, BLK, LAT + ROPE)
    tiled_queries = queries.reshape(TILES, TILE, head_count, LAT + ROPE)
    scale = (NOPE + ROPE) ** -0.5

    def one_tile(operands):
        tile_queries, tile_list, tile_count = operands
        key_rows = cache_blocks[tile_list].reshape(MAXB * BLK, LAT + ROPE)
        scores = jnp.einsum("qhc,kc->qhk", tile_queries.astype(jnp.float32), key_rows.astype(jnp.float32)) * scale
        slots = jnp.arange(MAXB)
        slot_of_key = jnp.repeat(slots, BLK)
        valid = (slot_of_key < tile_count)[None, None, :]
        shard_of = jnp.repeat(tile_list % N_CTX, BLK)[None, None, :]
        key_peak = jnp.full(scores.shape, -1e30, jnp.float32)
        for shard in range(N_CTX):
            selected = valid & (shard_of == shard)
            shard_peak = jnp.max(jnp.where(selected, scores, -1e30), axis=-1, keepdims=True)
            key_peak = jnp.where(selected, shard_peak, key_peak)
        global_peak = jnp.max(jnp.where(valid, scores, -1e30), axis=-1, keepdims=True)
        weights = jnp.where(valid, jnp.exp(scores - key_peak), 0.0).astype(jnp.bfloat16)
        scaled = weights.astype(jnp.float32) * jnp.where(valid, jnp.exp(key_peak - global_peak), 0.0)
        numerator = jnp.einsum("qhk,kl->qhl", scaled, key_rows[:, :LAT].astype(jnp.float32))
        mixed_latent = numerator / jnp.sum(scaled, axis=-1)[..., None]
        head_values = jnp.einsum("qhl,hlv->qhv", mixed_latent, w_absorb_value.astype(jnp.float32), precision=lax.Precision.HIGHEST)
        return head_values.astype(jnp.bfloat16)

    value_rows = lax.map(one_tile, (tiled_queries, block_lists, block_counts))
    flat_values = value_rows.reshape(TOKENS, head_count * VDIM)
    return jnp.dot(flat_values, w_output, preferred_element_type=jnp.float32).astype(jnp.bfloat16)
```

```python
import functools

import jax
import jax.numpy as jnp
import numpy as np
from jax import lax
from jax.experimental import pallas as pl
from jax.experimental.pallas import tpu as pltpu
from jax.sharding import PartitionSpec as P

LAT = 512
ROPE = 64
NOPE = 128
VDIM = 128
BLK = 64
TILE = 16
LMAX = 4
NEG = -1e30
LOG2E = 1.4426950408889634
MESH = pl.DeviceIdType.MESH
F32 = jnp.float32
BF16 = jnp.bfloat16


def dot_nt(a, b):
    return lax.dot_general(a, b, (((1,), (1,)), ((), ())), preferred_element_type=F32)


def dot_nn(a, b):
    return jnp.dot(a, b, preferred_element_type=F32)


def kernel(
    sizes,
    ql_hbm, wq_hbm, wr_hbm, wk_hbm, wv_hbm, wo_hbm, cache_hbm,
    lists_ref, counts_ref, pos_ref, freq_ref,
    out_ref,
    ql, wq, wr, wk, wv, wo, cache, rope_key,
    listbuf, scal, scal_smem, posbuf,
    qsend, qrecv, qabs, kstage, nabs,
    psend, precv, ssend, srecv, coef, vall, osend, orecv,
    in_sem, cache_sem, scal_sem,
    q_ss, q_rs, p_ss, p_rs, s_ss, s_rs, v_ss, v_rs, f_ss, f_rs, o_ss, o_rs,
):
    n_ctx, n_head, heads, tok, blocks, maxb, tiles = sizes
    peers = n_ctx // 2
    me_h = lax.axis_index("head")
    me_c = lax.axis_index("ctx")
    me8 = me_c // 2
    core = me_c % 2
    sibling = me8 * 2 + (1 - core)
    nope_w = heads * NOPE
    rope_w = heads * ROPE
    tiles_src = tok // TILE
    rows = heads * TILE
    keys = 2 * LMAX * BLK

    def same_core(offset):
        return (me8 + offset) % peers

    loads = [
        pltpu.make_async_copy(ql_hbm, ql, in_sem.at[0]),
        pltpu.make_async_copy(wq_hbm, wq, in_sem.at[1]),
        pltpu.make_async_copy(wr_hbm, wr, in_sem.at[2]),
        pltpu.make_async_copy(wk_hbm, wk, in_sem.at[3]),
        pltpu.make_async_copy(
            cache_hbm, cache.at[pl.ds(core * blocks, blocks)], in_sem.at[4]
        ),
        pltpu.make_async_copy(wv_hbm, wv, in_sem.at[5]),
        pltpu.make_async_copy(wo_hbm, wo, in_sem.at[6]),
    ]
    for load in loads:
        load.start()

    barrier = pltpu.get_barrier_semaphore()

    def greet_ctx(offset, carry):
        pl.semaphore_signal(
            barrier, inc=1, device_id=(me_h, same_core(offset) * 2 + core), device_id_type=MESH
        )
        return carry

    def greet_head(offset, carry):
        pl.semaphore_signal(
            barrier, inc=1, device_id=((me_h + offset) % n_head, me_c), device_id_type=MESH
        )
        return carry

    pl.semaphore_signal(barrier, inc=1, device_id=(me_h, sibling), device_id_type=MESH)
    lax.fori_loop(1, peers, greet_ctx, 0)
    lax.fori_loop(1, n_head, greet_head, 0)

    pos_row = pos_ref[pl.ds(me8, 1), :].astype(F32)
    posbuf[...] = jnp.transpose(jnp.broadcast_to(pos_row, (128, 128)))
    pos_col = posbuf[pl.ds(pl.multiple_of(core * tok, tok), tok), :]
    angle = pos_col * freq_ref[...]
    cosine = jnp.cos(angle)
    lane = lax.broadcasted_iota(jnp.int32, (tok, 128), 1)
    first_half = (lane % ROPE) < (ROPE // 2)
    sine = jnp.where(first_half, -jnp.sin(angle), jnp.sin(angle))

    loads[0].wait()
    loads[1].wait()
    latent = ql[...]
    chunk = 512
    for start in range(0, nope_w, chunk):
        qsend[:, start : start + chunk] = dot_nn(latent, wq[:, start : start + chunk]).astype(BF16)
    loads[2].wait()
    rope_part = dot_nn(latent, wr[...])
    for start in range(0, rope_w, 128):
        part = rope_part[:, start : start + 128]
        swapped = jnp.where(
            first_half,
            pltpu.roll(part, 128 - ROPE // 2, 1),
            pltpu.roll(part, ROPE // 2, 1),
        )
        qsend[:, nope_w + start : nope_w + start + 128] = (
            part * cosine + swapped * sine
        ).astype(BF16)

    pl.semaphore_wait(barrier, peers - 1 + 1 + n_head - 1)

    def q_copy(offset, slot):
        return pltpu.make_async_remote_copy(
            src_ref=qsend,
            dst_ref=qrecv.at[slot],
            send_sem=q_ss.at[offset],
            recv_sem=q_rs.at[slot],
            device_id=(me_h, same_core(offset) * 2 + core),
            device_id_type=MESH,
        )

    def q_start(offset, carry):
        q_copy(offset, me8).start()
        return carry

    lax.fori_loop(1, peers, q_start, 0)

    cache_copy = pltpu.make_async_remote_copy(
        src_ref=cache_hbm,
        dst_ref=cache.at[pl.ds(core * blocks, blocks)],
        send_sem=cache_sem.at[0],
        recv_sem=cache_sem.at[1],
        device_id=(me_h, sibling),
        device_id_type=MESH,
    )
    cache_copy.start()
    cache_in = pltpu.make_async_remote_copy(
        src_ref=cache_hbm,
        dst_ref=cache.at[pl.ds((1 - core) * blocks, blocks)],
        send_sem=cache_sem.at[0],
        recv_sem=cache_sem.at[1],
        device_id=(me_h, sibling),
        device_id_type=MESH,
    )

    own_q = pltpu.make_async_copy(qsend, qrecv.at[me8], in_sem.at[7])
    own_q.start()

    listbuf[...] = jnp.zeros_like(listbuf)
    listbuf[0:tiles, 0:maxb] = lists_ref[...]
    listbuf[...] = jnp.transpose(listbuf[...])
    counts = counts_ref[...]
    zero = jnp.zeros((1, tiles), jnp.int32)
    found = [zero, zero]
    index = [[zero] * LMAX, [zero] * LMAX]
    for slot in range(maxb):
        entry = listbuf[slot : slot + 1, 0:tiles]
        shard = entry % n_ctx
        local = entry // n_ctx
        valid = counts > slot
        for e in range(2):
            here = valid & (shard == me8 * 2 + e)
            for j in range(LMAX):
                index[e][j] = jnp.where(here & (found[e] == j), local + e * blocks, index[e][j])
            found[e] = found[e] + jnp.where(here, 1, 0)
    scal[...] = jnp.zeros_like(scal)
    for e in range(2):
        for j in range(LMAX):
            scal[e * LMAX + j : e * LMAX + j + 1, 0:tiles] = index[e][j]
        scal[2 * LMAX + e : 2 * LMAX + e + 1, 0:tiles] = found[e]
    scal_copy = pltpu.make_async_copy(scal, scal_smem, scal_sem)
    scal_copy.start()
    scal_copy.wait()

    loads[4].wait()
    cache_in.wait_recv()

    def double_key(b, carry):
        part = cache[b, :, LAT : LAT + ROPE]
        rope_key[b] = jnp.concatenate([part, part], axis=1)
        return carry

    lax.fori_loop(0, 2 * blocks, double_key, 0)

    loads[3].wait()
    loads[5].wait()
    own_q.wait()

    half_lane = lax.broadcasted_iota(jnp.int32, (1, 128), 1)
    half_mask = [
        (half_lane < ROPE).astype(F32).astype(BF16),
        (half_lane >= ROPE).astype(F32).astype(BF16),
    ]
    key_lane = lax.broadcasted_iota(jnp.int32, (1, keys), 1)
    key_slot = key_lane // BLK
    stat_lane = lax.broadcasted_iota(jnp.int32, (rows, 128), 1)
    scale = LOG2E * (NOPE + ROPE) ** (-0.5)

    def p_copy(offset, src_slot, slot):
        return pltpu.make_async_remote_copy(
            src_ref=psend.at[src_slot],
            dst_ref=precv.at[slot],
            send_sem=p_ss.at[offset],
            recv_sem=p_rs.at[slot],
            device_id=(me_h, same_core(offset) * 2 + core),
            device_id_type=MESH,
        )

    def s_copy(offset, src_slot, slot):
        return pltpu.make_async_remote_copy(
            src_ref=ssend.at[src_slot],
            dst_ref=srecv.at[slot],
            send_sem=s_ss.at[offset],
            recv_sem=s_rs.at[slot],
            device_id=(me_h, same_core(offset) * 2 + core),
            device_id_type=MESH,
        )

    def attend(src):
        for h in range(heads):
            nope = qrecv[src, :, h * NOPE : (h + 1) * NOPE]
            qabs[h, :, 0:LAT] = dot_nn(nope, wk[h]).astype(BF16)
            pair = qrecv[src, :, nope_w + (h // 2) * 128 : nope_w + (h // 2) * 128 + 128]
            qabs[h, :, LAT : LAT + 128] = pair * half_mask[h % 2]
        stats = jnp.zeros((rows, 128), F32)
        for i in range(tiles_src):
            tile = (src * 2 + core) * tiles_src + i
            for j in range(2 * LMAX):
                block = scal_smem[j, tile]
                kstage[i, j * BLK : (j + 1) * BLK, 0:LAT] = cache[block, :, 0:LAT]
                kstage[i, j * BLK : (j + 1) * BLK, LAT : LAT + 128] = rope_key[block]
            live_even = scal_smem[2 * LMAX, tile]
            live_odd = scal_smem[2 * LMAX + 1, tile]
            limit = jnp.where(key_slot < LMAX, live_even, live_odd + LMAX)
            bias = jnp.where(key_slot < limit, 0.0, NEG)
            query = qabs[:, i * TILE : (i + 1) * TILE, :].reshape(rows, LAT + 128)
            score = dot_nt(query, kstage[i]) * scale + bias
            peak = jnp.max(score, axis=1, keepdims=True)
            weight = jnp.exp2(score - peak)
            total = jnp.sum(weight, axis=1, keepdims=True)
            number = dot_nn(weight.astype(BF16), kstage[i, :, 0:LAT])
            nabs[:, i * TILE : (i + 1) * TILE, :] = number.astype(BF16).reshape(heads, TILE, LAT)
            stats = jnp.where(stat_lane == i, peak, stats)
            stats = jnp.where(stat_lane == tiles_src + i, total, stats)
        for h in range(heads):
            psend[src, h] = dot_nn(nabs[h], wv[h]).astype(BF16)
        ssend[src] = jnp.transpose(stats)[0 : 2 * tiles_src, :]

    attend(me8)

    def attend_peer(offset, carry):
        src = same_core(offset)
        q_copy(offset, src).wait_recv()
        attend(src)
        p_copy(offset, src, me8).start()
        s_copy(offset, src, me8).start()
        return carry

    lax.fori_loop(1, peers, attend_peer, 0)

    own_p = pltpu.make_async_copy(psend.at[me8], precv.at[me8], in_sem.at[8])
    own_s = pltpu.make_async_copy(ssend.at[me8], srecv.at[me8], in_sem.at[9])
    own_p.start()
    own_s.start()
    own_p.wait()
    own_s.wait()

    def p_wait(offset, carry):
        src = same_core(offset)
        s_copy(offset, src, src).wait_recv()
        p_copy(offset, src, src).wait_recv()
        return carry

    lax.fori_loop(1, peers, p_wait, 0)

    peaks = srecv[:, 0:tiles_src, :]
    sums = srecv[:, tiles_src : 2 * tiles_src, :]
    top = jnp.max(peaks, axis=0, keepdims=True)
    share = jnp.exp2(peaks - top)
    share = share / jnp.sum(share * sums, axis=0, keepdims=True)
    coef[...] = jnp.zeros_like(coef)
    for src in range(peers):
        coef[src * tiles_src : (src + 1) * tiles_src, :] = share[src]
    coef_t = jnp.transpose(coef[...])
    own = vall.at[me_c]
    for i in range(tiles_src):
        mixed = jnp.zeros((rows, VDIM), F32)
        for src in range(peers):
            column = coef_t[:, src * tiles_src + i : src * tiles_src + i + 1]
            part = precv[src, :, i * TILE : (i + 1) * TILE, :].astype(F32)
            mixed = mixed + column * part.reshape(rows, VDIM)
        mixed = mixed.astype(BF16).reshape(heads, TILE, VDIM)
        for h in range(heads):
            own[i * TILE : (i + 1) * TILE, h * VDIM : (h + 1) * VDIM] = mixed[h]

    def v_copy(offset, slot):
        return pltpu.make_async_remote_copy(
            src_ref=vall.at[me_c],
            dst_ref=vall.at[slot],
            send_sem=v_ss.at[offset],
            recv_sem=v_rs.at[slot // 2],
            device_id=(me_h, same_core(offset) * 2 + core),
            device_id_type=MESH,
        )

    def f_copy(offset, slot):
        return pltpu.make_async_remote_copy(
            src_ref=vall.at[slot],
            dst_ref=vall.at[slot],
            send_sem=f_ss.at[offset],
            recv_sem=f_rs.at[slot // 2],
            device_id=(me_h, sibling),
            device_id_type=MESH,
        )

    def o_copy(block, slot):
        return pltpu.make_async_remote_copy(
            src_ref=osend.at[block],
            dst_ref=orecv.at[slot],
            send_sem=o_ss.at[block],
            recv_sem=o_rs.at[slot],
            device_id=(block, me_c),
            device_id_type=MESH,
        )

    def v_start(offset, carry):
        v_copy(offset, me_c).start()
        return carry

    lax.fori_loop(1, peers, v_start, 0)
    f_copy(0, me_c).start()
    loads[6].wait()

    def project(block):
        osend[block] = dot_nn(vall[block], wo[...]).astype(BF16)

        @pl.when(block != me_h)
        def _():
            o_copy(block, me_h).start()

    project(me_c)

    def project_pair(offset, carry):
        src = same_core(offset)
        other = src * 2 + (1 - core)

        @pl.when(offset != 0)
        def _():
            v_copy(offset, src * 2 + core).wait_recv()
            f_copy(offset, src * 2 + core).start()
            project(src * 2 + core)

        f_copy(offset, other).wait_recv()
        project(other)
        return carry

    lax.fori_loop(0, peers, project_pair, 0)

    total = osend[me_h].astype(F32)

    def add_head(offset, total):
        src = (me_h + offset) % n_head
        o_copy(src, src).wait_recv()
        return total + orecv[src].astype(F32)

    total = lax.fori_loop(1, n_head, add_head, total)
    out_ref[...] = total.astype(BF16)

    cache_copy.wait_send()

    def drain_ctx(offset, carry):
        src = same_core(offset)
        q_copy(offset, me8).wait_send()
        p_copy(offset, src, me8).wait_send()
        s_copy(offset, src, me8).wait_send()
        v_copy(offset, me_c).wait_send()
        return carry

    lax.fori_loop(1, peers, drain_ctx, 0)

    def drain_sibling(offset, carry):
        f_copy(offset, same_core(offset) * 2 + core).wait_send()
        return carry

    lax.fori_loop(0, peers, drain_sibling, 0)

    def drain_head(offset, carry):
        o_copy((me_h + offset) % n_head, me_h).wait_send()
        return carry

    lax.fori_loop(1, n_head, drain_head, 0)


def local(
    n_ctx, n_head,
    query_latent, w_query_nope, w_query_rope, w_absorb_key, w_absorb_value, w_output,
    latent_cache, block_lists, block_counts, positions,
):
    tok, q_lat = query_latent.shape
    heads = w_absorb_key.shape[0]
    blocks = latent_cache.shape[0]
    tiles, maxb = block_lists.shape
    cols = w_output.shape[1]
    peers = n_ctx // 2
    tiles_src = tok // TILE
    nope_w = heads * NOPE
    rope_w = heads * ROPE
    rows = heads * TILE
    keys = 2 * LMAX * BLK
    half = ROPE // 2
    frequency = 10000.0 ** (-2.0 * np.arange(half, dtype=np.float64) / ROPE)
    frequency = np.tile(frequency.astype(np.float32), 128 // half)[None, :]
    sizes = (n_ctx, n_head, heads, tok, blocks, maxb, tiles)
    hbm = pl.BlockSpec(memory_space=pl.ANY)
    vmem = pl.BlockSpec(memory_space=pltpu.VMEM)
    dma = pltpu.SemaphoreType.DMA
    return pl.pallas_call(
        functools.partial(kernel, sizes),
        out_shape=jax.ShapeDtypeStruct((tok, cols), BF16),
        in_specs=[hbm] * 7 + [vmem] * 4,
        out_specs=vmem,
        scratch_shapes=[
            pltpu.VMEM((tok, q_lat), BF16),
            pltpu.VMEM((q_lat, nope_w), BF16),
            pltpu.VMEM((q_lat, rope_w), BF16),
            pltpu.VMEM((heads, NOPE, LAT), BF16),
            pltpu.VMEM((heads, LAT, VDIM), BF16),
            pltpu.VMEM((heads * VDIM, cols), BF16),
            pltpu.VMEM((2 * blocks, BLK, LAT + ROPE), BF16),
            pltpu.VMEM((2 * blocks, BLK, 128), BF16),
            pltpu.VMEM((128, 128), jnp.int32),
            pltpu.VMEM((16, 128), jnp.int32),
            pltpu.SMEM((16, 128), jnp.int32),
            pltpu.VMEM((128, 128), F32),
            pltpu.VMEM((tok, nope_w + rope_w), BF16),
            pltpu.VMEM((peers, tok, nope_w + rope_w), BF16),
            pltpu.VMEM((heads, tok, LAT + 128), BF16),
            pltpu.VMEM((tiles_src, keys, LAT + 128), BF16),
            pltpu.VMEM((heads, tok, LAT), BF16),
            pltpu.VMEM((peers, heads, tok, VDIM), BF16),
            pltpu.VMEM((peers, heads, tok, VDIM), BF16),
            pltpu.VMEM((peers, 2 * tiles_src, 128), F32),
            pltpu.VMEM((peers, 2 * tiles_src, 128), F32),
            pltpu.VMEM((128, 128), F32),
            pltpu.VMEM((n_ctx, tok, nope_w), BF16),
            pltpu.VMEM((n_head, tok, cols), BF16),
            pltpu.VMEM((n_head, tok, cols), BF16),
            dma((10,)),
            dma((2,)),
            dma(()),
            dma((peers,)),
            dma((peers,)),
            dma((peers,)),
            dma((peers,)),
            dma((peers,)),
            dma((peers,)),
            dma((peers,)),
            dma((peers,)),
            dma((peers,)),
            dma((peers,)),
            dma((n_head,)),
            dma((n_head,)),
        ],
        compiler_params=pltpu.CompilerParams(
            collective_id=0, has_side_effects=True, vmem_limit_bytes=48 * 1024 * 1024
        ),
    )(
        query_latent, w_query_nope, w_query_rope, w_absorb_key, w_absorb_value, w_output,
        latent_cache, block_lists, block_counts.reshape(1, tiles),
        positions.reshape(positions.shape[0] // 128, 128), jnp.asarray(frequency),
    )


def solution(mesh):
    in_specs = (
        P("ctx", None),
        P(None, "head"),
        P(None, "head"),
        P("head", None, None),
        P("head", None, None),
        P("head", "ctx"),
        P(None, "ctx", None),
        P(),
        P(),
        P(),
    )
    run = functools.partial(local, mesh.shape["ctx"], mesh.shape["head"])
    return jax.shard_map(
        run, mesh=mesh, in_specs=in_specs, out_specs=P("head", "ctx"), check_vma=False
    )
```

```python
import functools

import jax
import jax.numpy as jnp
import numpy as np
from jax import lax
from jax.experimental import pallas as pl
from jax.experimental.pallas import tpu as pltpu
from jax.sharding import PartitionSpec as P

LAT = 512
ROPE = 64
NOPE = 128
VDIM = 128
BLK = 64
TILE = 16
LMAX = 4
NEG = -1e30
PARTS = 4
LOG2E = 1.4426950408889634
MESH = pl.DeviceIdType.MESH
F32 = jnp.float32
BF16 = jnp.bfloat16


def dot_nt(a, b):
    return lax.dot_general(a, b, (((1,), (1,)), ((), ())), preferred_element_type=F32)


def dot_nn(a, b):
    return jnp.dot(a, b, preferred_element_type=F32)


def kernel(
    sizes,
    ql_hbm, wq_hbm, wr_hbm, wk_hbm, wv_hbm, wo_hbm, cache_hbm,
    lists_hbm, counts_hbm, pos_hbm, freq_hbm,
    out_ref,
    ql, wq, wr, wk, wv, wo, cache, rope_key,
    lists_ref, counts_ref, pos_ref, freq_ref, scal, scal_smem, posbuf,
    qrecv, qabs, kstage, nabs,
    psend, precv, ssend, srecv, coef, vown, vall, osend, orecv,
    in_sem, ex_ss, ex_rs, scal_sem,
    q_ss, q_rs, r_ss, p_ss, p_rs, s_ss, s_rs, v_ss, v_rs, o_ss, o_rs,
):
    n_ctx, n_head, heads, tok, blocks, maxb, tiles, parts = sizes
    peers = n_ctx // 2
    n_y = peers // 2
    me_h = lax.axis_index("head")
    me_c = lax.axis_index("ctx")
    me8 = me_c // 2
    core = me_c % 2
    me_y = me8 // 2
    me_x = me8 % 2
    me_z = me_h // 2
    lo = me_h % 2
    sibling = (me_h, me8 * 2 + (1 - core))
    across = (me_z * 2 + (1 - lo), me_c)
    nope_w = heads * NOPE
    rope_w = heads * ROPE
    tiles_src = tok // TILE
    tiles_part = tiles_src // parts
    tok_part = tok // parts
    rows = heads * TILE
    keys = 2 * LMAX * BLK

    def shift_of(pair, g):
        middle = ((pair + 1) // 2) % 2
        dx = middle * (pair // 2) + (1 - middle) * g
        dy = middle * (3 - 2 * g) + (1 - middle) * 2 * (pair // 3)
        return dy, dx

    def peer8(pair, g):
        dy, dx = shift_of(pair, g)
        return ((me_y + dy) % n_y) * 2 + (me_x + dx) % 2

    def peer(pair, g):
        return (me_h, peer8(pair, g) * 2 + core)

    def mirror(pair, g):
        middle = ((pair + 1) // 2) % 2
        return 2 * pair + middle * (1 - g) + (1 - middle) * g

    small = [
        pltpu.make_async_copy(pos_hbm, pos_ref, in_sem.at[7]),
        pltpu.make_async_copy(freq_hbm, freq_ref, in_sem.at[8]),
        pltpu.make_async_copy(lists_hbm, lists_ref, in_sem.at[9]),
        pltpu.make_async_copy(counts_hbm, counts_ref, in_sem.at[10]),
    ]
    loads = [
        pltpu.make_async_copy(ql_hbm, ql, in_sem.at[0]),
        pltpu.make_async_copy(wq_hbm, wq, in_sem.at[1]),
        pltpu.make_async_copy(wr_hbm, wr, in_sem.at[2]),
        pltpu.make_async_copy(
            cache_hbm, cache.at[pl.ds(core * blocks, blocks)], in_sem.at[3]
        ),
        pltpu.make_async_copy(wk_hbm, wk, in_sem.at[4]),
        pltpu.make_async_copy(wv_hbm, wv, in_sem.at[5]),
        pltpu.make_async_copy(wo_hbm, wo.at[0, core], in_sem.at[6]),
    ]
    for load in small + loads:
        load.start()

    barrier = pltpu.get_barrier_semaphore()

    def greet(device):
        pl.semaphore_signal(barrier, inc=1, device_id=device, device_id_type=MESH)

    def greet_peers(pair, carry):
        for g in range(2):

            @pl.when(2 * pair + g != 0)
            def _():
                greet(peer(pair, g))

        return carry

    def value_source(n, other):
        return (me_z * 2 + other, (n * 2 + core) * 2 + lo)

    def greet_value_sources(n, carry):
        for other in range(2):

            @pl.when((n != me_y) | (other != lo) | (core != me_x) | (lo != core))
            def _():
                greet(value_source(n, other))

        return carry

    def greet_planes(n, carry):
        @pl.when((n != me_z) | (me_z % 2 != core))
        def _():
            greet((n * 2 + lo, me8 * 2 + me_z % 2))

        return carry

    greet(sibling)
    greet(across)
    lax.fori_loop(0, peers // 2, greet_peers, 0)
    lax.fori_loop(0, n_y, greet_value_sources, 0)
    lax.fori_loop(0, peers, greet_planes, 0)

    small[0].wait()
    small[1].wait()
    pos_row = pos_ref[pl.ds(me8, 1), :].astype(F32)
    posbuf[...] = jnp.transpose(jnp.broadcast_to(pos_row, (128, 128)))
    pos_col = posbuf[pl.ds(pl.multiple_of(core * tok, tok), tok), :]
    angle = pos_col * freq_ref[...]
    cosine = jnp.cos(angle)
    lane = lax.broadcasted_iota(jnp.int32, (tok, 128), 1)
    first_half = (lane % ROPE) < (ROPE // 2)
    sine = jnp.where(first_half, -jnp.sin(angle), jnp.sin(angle))

    loads[0].wait()
    loads[1].wait()
    latent = ql[...]
    chunk = 512
    for start in range(0, nope_w, chunk):
        qrecv[0, :, start : start + chunk] = dot_nn(
            latent, wq[:, start : start + chunk]
        ).astype(BF16)
    loads[2].wait()
    rope_part = dot_nn(latent, wr[...])
    for start in range(0, rope_w, 128):
        part = rope_part[:, start : start + 128]
        swapped = jnp.where(
            first_half,
            pltpu.roll(part, 128 - ROPE // 2, 1),
            pltpu.roll(part, ROPE // 2, 1),
        )
        qrecv[0, :, nope_w + start : nope_w + start + 128] = (
            part * cosine + swapped * sine
        ).astype(BF16)

    small[2].wait()
    small[3].wait()
    counts = counts_ref[...]
    zero = jnp.zeros((1, tiles), jnp.int32)
    found = [zero, zero]
    index = [[zero] * LMAX, [zero] * LMAX]
    for slot in range(maxb):
        entry = lists_ref[slot : slot + 1, :]
        shard = entry % n_ctx
        local = entry // n_ctx
        valid = counts > slot
        for e in range(2):
            here = valid & (shard == me8 * 2 + e)
            for j in range(LMAX):
                index[e][j] = jnp.where(here & (found[e] == j), local + e * blocks, index[e][j])
            found[e] = found[e] + jnp.where(here, 1, 0)
    scal[...] = jnp.zeros_like(scal)
    for e in range(2):
        for j in range(LMAX):
            scal[e * LMAX + j : e * LMAX + j + 1, 0:tiles] = index[e][j]
        scal[2 * LMAX + e : 2 * LMAX + e + 1, 0:tiles] = found[e]
    scal_copy = pltpu.make_async_copy(scal, scal_smem, scal_sem)
    scal_copy.start()

    loads[3].wait()

    def double_key(b, carry):
        part = cache[core * blocks + b, :, LAT : LAT + ROPE]
        rope_key[core * blocks + b] = jnp.concatenate([part, part], axis=1)
        return carry

    lax.fori_loop(0, blocks, double_key, 0)

    scal_copy.wait()
    self_value = (1 - (core + lo) % 2) * (1 - (core + me_x) % 2)
    self_plane = 1 - (me_z + core) % 2
    pl.semaphore_wait(barrier, peers - 1 + 2 + peers - self_value + peers - self_plane)

    def remote(src, dst, send_sem, recv_sem, device):
        return pltpu.make_async_remote_copy(
            src_ref=src,
            dst_ref=dst,
            send_sem=send_sem,
            recv_sem=recv_sem,
            device_id=device,
            device_id_type=MESH,
        )

    def q_copy(held, pair, g, slot, send_sem):
        return remote(qrecv.at[held], qrecv.at[slot], send_sem, q_rs.at[slot], peer(pair, g))

    first_q = [q_copy(0, 0, 1, 1, q_ss.at[0])]
    relay_q = []
    last_q = []
    if n_y == 4:
        first_q += [q_copy(0, 1, g, mirror(1, g), q_ss.at[1 + g]) for g in range(2)]
        relay_q = [q_copy(1, 1, g, mirror(2, g), r_ss.at[g]) for g in range(2)]
        last_q = [
            q_copy(2 + me_x, 1, 1 - me_x, 6, r_ss.at[2]),
            q_copy(5 - me_x, 1, me_x, 7, r_ss.at[3]),
        ]
    for copy in first_q:
        copy.start()

    def exchange(which, src, dst, device):
        return remote(src, dst, ex_ss.at[which], ex_rs.at[which], device)

    def exchanges(side):
        half = pl.ds(side * blocks, blocks)
        own = pl.ds(core * blocks, blocks)
        return [
            exchange(0, cache_hbm, cache.at[half], sibling),
            exchange(1, rope_key.at[own], rope_key.at[half], sibling),
            exchange(2, wo_hbm, wo.at[0, side], sibling),
            exchange(3, wo_hbm, wo.at[1, core], across),
            exchange(4, wo.at[1, core], wo.at[1, side], sibling),
        ]

    swaps_out = exchanges(core)
    swaps_in = exchanges(1 - core)
    swaps_in[3] = swaps_out[3]
    for swap in swaps_out[:3]:
        swap.start()

    pairs = peers // 2
    seats = min(2, pairs)
    half_lane = lax.broadcasted_iota(jnp.int32, (1, 128), 1)
    half_mask = [
        (half_lane < ROPE).astype(F32).astype(BF16),
        (half_lane >= ROPE).astype(F32).astype(BF16),
    ]
    key_lane = lax.broadcasted_iota(jnp.int32, (1, keys), 1)
    key_slot = key_lane // BLK
    stat_lane = lax.broadcasted_iota(jnp.int32, (rows, 128), 1)
    scale = LOG2E * (NOPE + ROPE) ** (-0.5)

    loads[4].wait()

    def absorb(pair):
        group, first = 2, 2 * pair
        span = pl.ds(first, group)
        spot = pl.ds(pl.multiple_of(first * tok, tok), group * tok)
        for h in range(heads):
            nope = qrecv[span, :, h * NOPE : (h + 1) * NOPE].reshape(group * tok, NOPE)
            qabs[h, spot, 0:LAT] = dot_nn(nope, wk[h]).astype(BF16)
            start = nope_w + (h // 2) * 128
            pair = qrecv[span, :, start : start + 128].reshape(group * tok, 128)
            qabs[h, spot, LAT : LAT + 128] = pair * half_mask[h % 2]

    def attend(pair, part, seat):
        for g in range(2):
            slot = 2 * pair + g
            src = peer8(pair, g) * 2 + core
            stats = jnp.zeros((rows, 128), F32)
            for i in range(tiles_part):
                tile = src * tiles_src + part * tiles_part + i
                stage = (2 * seat + g) * tiles_part + i
                for j in range(2 * LMAX):
                    block = scal_smem[j, tile]
                    kstage[stage, j * BLK : (j + 1) * BLK, 0:LAT] = cache[block, :, 0:LAT]
                    kstage[stage, j * BLK : (j + 1) * BLK, LAT : LAT + 128] = rope_key[block]
                live_even = scal_smem[2 * LMAX, tile]
                live_odd = scal_smem[2 * LMAX + 1, tile]
                limit = jnp.where(key_slot < LMAX, live_even, live_odd + LMAX)
                bias = jnp.where(key_slot < limit, 0.0, NEG)
                start = pl.multiple_of(slot * tok + part * tok_part + i * TILE, TILE)
                query = qabs[:, pl.ds(start, TILE), :].reshape(rows, LAT + 128)
                score = dot_nt(query, kstage[stage]) * scale + bias
                peak = jnp.max(score, axis=1, keepdims=True)
                weight = jnp.exp2(score - peak)
                total = jnp.sum(weight, axis=1, keepdims=True)
                number = dot_nn(weight.astype(BF16), kstage[stage, :, 0:LAT])
                place = (2 * seat + g) * tok_part + i * TILE
                nabs[:, place : place + TILE, :] = number.astype(BF16).reshape(heads, TILE, LAT)
                stats = jnp.where(stat_lane == i, peak, stats)
                stats = jnp.where(stat_lane == tiles_part + i, total, stats)
            ssend[part, slot] = jnp.transpose(stats)[0:8, :]

    def p_copy(part, pair, g, slot):
        held = 2 * pair + g
        return remote(
            psend.at[part, held], precv.at[part, slot],
            p_ss.at[part, held], p_rs.at[part, slot], peer(pair, g),
        )

    def s_copy(part, pair, g, slot):
        held = 2 * pair + g
        return remote(
            ssend.at[part, held], srecv.at[part, slot],
            s_ss.at[part, held], s_rs.at[part, slot], peer(pair, g),
        )

    def send_values(pair, part, seats, seat):
        start = 2 * seat * tok_part
        count = 2 * seats * tok_part
        for h in range(heads):
            value = dot_nn(nabs[h, start : start + count], wv[h]).astype(BF16)
            for n in range(2 * seats):
                psend[part, 2 * pair + n, h] = value[n * tok_part : (n + 1) * tok_part, :]
        for n in range(2 * seats):
            now, g = pair + n // 2, n % 2

            @pl.when(2 * now + g != 0)
            def _():
                s_copy(part, now, g, mirror(now, g)).start()
                p_copy(part, now, g, mirror(now, g)).start()

    def q_wait(slot):
        q_copy(0, 0, 1, slot, q_ss.at[0]).wait_recv()

    def attend_new(pair, carry):
        for g in range(2):

            @pl.when(2 * pair + g != 0)
            def _():
                q_wait(2 * pair + g)

        @pl.when(pair == 0)
        def _():
            for copy in relay_q:
                copy.start()
            swaps_out[3].start()

        if n_y == 4:

            @pl.when(pair == 1)
            def _():
                last_q[0].start()

            @pl.when(pair == 2)
            def _():
                last_q[1].start()

        absorb(pair)

        @pl.when(pair == 0)
        def _():
            loads[5].wait()
            swaps_in[0].wait_recv()
            swaps_in[1].wait_recv()

        for part in range(2):
            attend(pair, part, part)
        for part in range(2):
            send_values(pair, part, 1, part)
        return carry

    def attend_again(part, seats):
        def step(n, carry):
            first = pairs - (n + 1) * seats
            for seat in range(seats):
                attend(first + seat, part, seat)
            send_values(first, part, seats, 0)
            return carry

        return step

    def combine(part):
        def p_wait(slot, carry):
            s_copy(part, 0, 0, slot).wait_recv()
            p_copy(part, 0, 0, slot).wait_recv()
            return carry

        lax.fori_loop(1, peers, p_wait, 0)
        srecv[part, 0] = ssend[part, 0]
        peaks = srecv[part, :, 0:tiles_part, :]
        sums = srecv[part, :, tiles_part : 2 * tiles_part, :]
        top = jnp.max(peaks, axis=0, keepdims=True)
        share = jnp.exp2(peaks - top)
        share = share / jnp.sum(share * sums, axis=0, keepdims=True)
        coef[...] = jnp.zeros_like(coef)
        for src in range(peers):
            coef[src * tiles_part : (src + 1) * tiles_part, :] = share[src]
        coef_t = jnp.transpose(coef[...])
        for i in range(tiles_part):
            mixed = jnp.zeros((rows, VDIM), F32)
            for src in range(peers):
                column = coef_t[:, src * tiles_part + i : src * tiles_part + i + 1]
                held = psend if src == 0 else precv
                term = held[part, src, :, i * TILE : (i + 1) * TILE, :].astype(F32)
                mixed = mixed + column * term.reshape(rows, VDIM)
            mixed = mixed.astype(BF16).reshape(heads, TILE, VDIM)
            for h in range(heads):
                vown[part, i * TILE : (i + 1) * TILE, h * VDIM : (h + 1) * VDIM] = mixed[h]

    def v_copy(part, n, slot):
        target = ((me_y + n // 2) % n_y) * 2 + (me_x + n) % 2
        return remote(
            vown.at[part], vall.at[part, slot // n_y, slot % n_y],
            v_ss.at[part, n], v_rs.at[part, slot],
            (me_z * 2 + core, target * 2 + me_x),
        )

    my_slot = lo * n_y + me_y

    def keeps(n):
        return (n == 0) & (core == lo) & (core == me_x)

    def gather(part):
        def v_start(n, carry):
            @pl.when(keeps(n))
            def _():
                vall[part, lo, me_y] = vown[part]

            @pl.when(jnp.logical_not(keeps(n)))
            def _():
                v_copy(part, n, my_slot).start()

            return carry

        lax.fori_loop(0, peers, v_start, 0)

    def o_copy(part, n, e, slot):
        plane = 2 * n + core
        return remote(
            osend.at[part, n, e], orecv.at[part, slot],
            o_ss.at[part, n, e], o_rs.at[part, slot],
            (plane * 2 + lo, me8 * 2 + e),
        )

    def stays(n, e):
        return (2 * n + core == me_z) & (core == e)

    def project(part):
        def v_wait(slot, carry):
            @pl.when(
                (slot != my_slot) | (core != lo) | (core != me_x)
            )
            def _():
                v_copy(part, 0, slot).wait_recv()

            return carry

        lax.fori_loop(0, peers, v_wait, 0)
        for e in range(2):
            product = dot_nt(vall[part, lo].reshape(n_y * tok_part, nope_w), wo[0, e])
            product = product + dot_nt(
                vall[part, 1 - lo].reshape(n_y * tok_part, nope_w), wo[1, e]
            )
            product = product.astype(BF16)
            for n in range(n_y):
                osend[part, n, e] = product[n * tok_part : (n + 1) * tok_part, :]

        def o_start(n, carry):
            at = (n + me_z // 2) % n_y
            for e in range(2):

                @pl.when(stays(at, e))
                def _():
                    orecv[part, me_z] = osend[part, at, e]

                @pl.when(jnp.logical_not(stays(at, e)))
                def _():
                    o_copy(part, at, e, me_z).start()

            return carry

        lax.fori_loop(0, n_y, o_start, 0)

    def collect(part):
        @pl.when(me_z % 2 != core)
        def _():
            o_copy(part, 0, 0, me_z).wait_recv()

        total = orecv[part, me_z].astype(F32)

        def add_plane(n, total):
            src = (me_z + n) % peers
            o_copy(part, 0, 0, src).wait_recv()
            return total + orecv[part, src].astype(F32)

        total = lax.fori_loop(1, peers, add_plane, total)
        out_ref[part * tok_part : (part + 1) * tok_part, :] = total.astype(BF16)

    lax.fori_loop(0, pairs, attend_new, 0)
    lax.fori_loop(0, pairs // seats, attend_again(2, seats), 0)
    for part in range(2):
        combine(part)
        gather(part)
    lax.fori_loop(0, pairs // seats, attend_again(3, seats), 0)
    combine(2)
    gather(2)
    loads[6].wait()
    swaps_in[2].wait_recv()
    swaps_in[3].wait_recv()
    swaps_out[4].start()
    swaps_in[4].wait_recv()
    project(0)
    project(1)
    combine(3)
    gather(3)
    project(2)
    project(3)
    for part in range(parts):
        collect(part)

    for swap in swaps_out:
        swap.wait_send()

    for copy in first_q + relay_q + last_q:
        copy.wait_send()

    def drain_peers(pair, carry):
        for g in range(2):

            @pl.when(2 * pair + g != 0)
            def _():
                for part in range(parts):
                    p_copy(part, pair, g, 0).wait_send()
                    s_copy(part, pair, g, 0).wait_send()

        return carry

    lax.fori_loop(0, pairs, drain_peers, 0)

    def drain_values(n, carry):
        @pl.when(jnp.logical_not(keeps(n)))
        def _():
            for part in range(parts):
                v_copy(part, n, my_slot).wait_send()

        return carry

    lax.fori_loop(0, peers, drain_values, 0)

    def drain_planes(n, carry):
        for e in range(2):

            @pl.when(jnp.logical_not(stays(n, e)))
            def _():
                for part in range(parts):
                    o_copy(part, n, e, me_z).wait_send()

        return carry

    lax.fori_loop(0, n_y, drain_planes, 0)


def local(
    n_ctx, n_head,
    query_latent, w_query_nope, w_query_rope, w_absorb_key, w_absorb_value, w_output,
    latent_cache, block_lists, block_counts, positions,
):
    tok, q_lat = query_latent.shape
    heads = w_absorb_key.shape[0]
    blocks = latent_cache.shape[0]
    tiles, maxb = block_lists.shape
    cols = w_output.shape[1]
    peers = n_ctx // 2
    tiles_src = tok // TILE
    nope_w = heads * NOPE
    rope_w = heads * ROPE
    rows = heads * TILE
    keys = 2 * LMAX * BLK
    half = ROPE // 2
    frequency = 10000.0 ** (-2.0 * np.arange(half, dtype=np.float64) / ROPE)
    frequency = np.tile(frequency.astype(np.float32), 128 // half)[None, :]
    parts = PARTS
    n_y = peers // 2
    tok_part = tok // parts
    sizes = (n_ctx, n_head, heads, tok, blocks, maxb, tiles, parts)
    hbm = pl.BlockSpec(memory_space=pltpu.HBM)
    vmem = pl.BlockSpec(memory_space=pltpu.VMEM)
    dma = pltpu.SemaphoreType.DMA
    return pl.pallas_call(
        functools.partial(kernel, sizes),
        out_shape=jax.ShapeDtypeStruct((tok, cols), BF16),
        in_specs=[hbm] * 11,
        out_specs=vmem,
        scratch_shapes=[
            pltpu.VMEM((tok, q_lat), BF16),
            pltpu.VMEM((q_lat, nope_w), BF16),
            pltpu.VMEM((q_lat, rope_w), BF16),
            pltpu.VMEM((heads, NOPE, LAT), BF16),
            pltpu.VMEM((heads, LAT, VDIM), BF16),
            pltpu.VMEM((2, 2, cols, heads * VDIM), BF16),
            pltpu.VMEM((2 * blocks, BLK, LAT + ROPE), BF16),
            pltpu.VMEM((2 * blocks, BLK, 128), BF16),
            pltpu.VMEM((maxb, tiles), jnp.int32),
            pltpu.VMEM((1, tiles), jnp.int32),
            pltpu.VMEM((positions.shape[0] // 128, 128), jnp.int32),
            pltpu.VMEM((1, 128), F32),
            pltpu.VMEM((16, 128), jnp.int32),
            pltpu.SMEM((16, 128), jnp.int32),
            pltpu.VMEM((128, 128), F32),
            pltpu.VMEM((peers, tok, nope_w + rope_w), BF16),
            pltpu.VMEM((heads, peers * tok, LAT + 128), BF16),
            pltpu.VMEM((4 * tiles_src // parts, keys, LAT + 128), BF16),
            pltpu.VMEM((heads, 4 * tok_part, LAT), BF16),
            pltpu.VMEM((parts, peers, heads, tok_part, VDIM), BF16),
            pltpu.VMEM((parts, peers, heads, tok_part, VDIM), BF16),
            pltpu.VMEM((parts, peers, 8, 128), F32),
            pltpu.VMEM((parts, peers, 8, 128), F32),
            pltpu.VMEM((128, 128), F32),
            pltpu.VMEM((parts, tok_part, nope_w), BF16),
            pltpu.VMEM((parts, 2, n_y, tok_part, nope_w), BF16),
            pltpu.VMEM((parts, n_y, 2, tok_part, cols), BF16),
            pltpu.VMEM((parts, peers, tok_part, cols), BF16),
            dma((11,)),
            dma((5,)),
            dma((5,)),
            dma(()),
            dma((3,)),
            dma((peers,)),
            dma((4,)),
            dma((parts, peers)),
            dma((parts, peers)),
            dma((parts, peers)),
            dma((parts, peers)),
            dma((parts, peers)),
            dma((parts, peers)),
            dma((parts, n_y, 2)),
            dma((parts, peers)),
        ],
        compiler_params=pltpu.CompilerParams(
            collective_id=0, has_side_effects=True, vmem_limit_bytes=63 * 1024 * 1024
        ),
    )(
        query_latent, w_query_nope, w_query_rope, w_absorb_key, w_absorb_value, w_output.T,
        latent_cache, block_lists.T, block_counts.reshape(1, tiles),
        positions.reshape(positions.shape[0] // 128, 128), jnp.asarray(frequency),
    )


def solution(mesh):
    in_specs = (
        P("ctx", None),
        P(None, "head"),
        P(None, "head"),
        P("head", None, None),
        P("head", None, None),
        P("head", "ctx"),
        P(None, "ctx", None),
        P(),
        P(),
        P(),
    )
    run = functools.partial(local, mesh.shape["ctx"], mesh.shape["head"])
    return jax.shard_map(
        run, mesh=mesh, in_specs=in_specs, out_specs=P("head", "ctx"), check_vma=False
    )
```

```python
import functools

import jax
import jax.numpy as jnp
import numpy as np
from jax import lax
from jax.experimental import pallas as pl
from jax.experimental.pallas import tpu as pltpu
from jax.sharding import PartitionSpec as P

LAT = 512
ROPE = 64
NOPE = 128
VDIM = 128
BLK = 64
TILE = 16
LMAX = 4
NEG = -1e30
PARTS = 4
LOG2E = 1.4426950408889634
MESH = pl.DeviceIdType.MESH
F32 = jnp.float32
BF16 = jnp.bfloat16


def dot_nt(a, b):
    return lax.dot_general(a, b, (((1,), (1,)), ((), ())), preferred_element_type=F32)


def dot_nn(a, b):
    return jnp.dot(a, b, preferred_element_type=F32)


def kernel(
    sizes,
    ql_hbm, wq_hbm, wr_hbm, wk_hbm, wv_hbm, wo_hbm, cache_hbm,
    lists_hbm, counts_hbm, pos_hbm, freq_hbm,
    out_ref,
    ql, wq, wr, wk, wv, wo, cache, rope_key,
    lists_ref, counts_ref, pos_ref, freq_ref, scal, scal_smem, posbuf,
    qrecv, qabs, kstage, nabs,
    psend, precv, ssend, srecv, coef, vown, vall, osend, orecv,
    in_sem, ex_ss, ex_rs, scal_sem,
    q_ss, q_rs, r_ss, p_ss, p_rs, s_ss, s_rs, v_ss, v_rs, o_ss, o_rs,
):
    n_ctx, n_head, heads, tok, blocks, maxb, tiles, parts = sizes
    peers = n_ctx // 2
    n_y = peers // 2
    me_h = lax.axis_index("head")
    me_c = lax.axis_index("ctx")
    me8 = me_c // 2
    core = me_c % 2
    me_y = me8 // 2
    me_x = me8 % 2
    me_z = me_h // 2
    lo = me_h % 2
    sibling = (me_h, me8 * 2 + (1 - core))
    across = (me_z * 2 + (1 - lo), me_c)
    nope_w = heads * NOPE
    rope_w = heads * ROPE
    tiles_src = tok // TILE
    tiles_part = tiles_src // parts
    tok_part = tok // parts
    rows = heads * TILE
    keys = 2 * LMAX * BLK

    def shift_of(pair, g):
        middle = ((pair + 1) // 2) % 2
        dx = middle * (pair // 2) + (1 - middle) * g
        dy = middle * (3 - 2 * g) + (1 - middle) * 2 * (pair // 3)
        return dy, dx

    def peer8(pair, g):
        dy, dx = shift_of(pair, g)
        return ((me_y + dy) % n_y) * 2 + (me_x + dx) % 2

    def peer(pair, g):
        return (me_h, peer8(pair, g) * 2 + core)

    def mirror(pair, g):
        middle = ((pair + 1) // 2) % 2
        return 2 * pair + middle * (1 - g) + (1 - middle) * g

    small = [
        pltpu.make_async_copy(pos_hbm, pos_ref, in_sem.at[7]),
        pltpu.make_async_copy(freq_hbm, freq_ref, in_sem.at[8]),
        pltpu.make_async_copy(lists_hbm, lists_ref, in_sem.at[9]),
        pltpu.make_async_copy(counts_hbm, counts_ref, in_sem.at[10]),
    ]
    loads = [
        pltpu.make_async_copy(ql_hbm, ql, in_sem.at[0]),
        pltpu.make_async_copy(wq_hbm, wq, in_sem.at[1]),
        pltpu.make_async_copy(wr_hbm, wr, in_sem.at[2]),
        pltpu.make_async_copy(
            cache_hbm, cache.at[pl.ds(core * blocks, blocks)], in_sem.at[3]
        ),
        pltpu.make_async_copy(wk_hbm, wk, in_sem.at[4]),
        pltpu.make_async_copy(wv_hbm, wv, in_sem.at[5]),
        pltpu.make_async_copy(wo_hbm, wo.at[0, core], in_sem.at[6]),
    ]
    for load in small + loads:
        load.start()

    barrier = pltpu.get_barrier_semaphore()

    def greet(device):
        pl.semaphore_signal(barrier, inc=1, device_id=device, device_id_type=MESH)

    def greet_peers(pair, carry):
        for g in range(2):

            @pl.when(2 * pair + g != 0)
            def _():
                greet(peer(pair, g))

        return carry

    def value_source(n, other):
        return (me_z * 2 + other, (n * 2 + core) * 2 + lo)

    def greet_value_sources(n, carry):
        for other in range(2):

            @pl.when((n != me_y) | (other != lo) | (core != me_x) | (lo != core))
            def _():
                greet(value_source(n, other))

        return carry

    def greet_planes(n, carry):
        @pl.when((n != me_z) | (me_z % 2 != core))
        def _():
            greet((n * 2 + lo, me8 * 2 + me_z % 2))

        return carry

    greet(sibling)
    greet(across)
    lax.fori_loop(0, peers // 2, greet_peers, 0)
    lax.fori_loop(0, n_y, greet_value_sources, 0)
    lax.fori_loop(0, peers, greet_planes, 0)

    small[0].wait()
    small[1].wait()
    pos_row = pos_ref[pl.ds(me8, 1), :].astype(F32)
    posbuf[...] = jnp.transpose(jnp.broadcast_to(pos_row, (128, 128)))
    pos_col = posbuf[pl.ds(pl.multiple_of(core * tok, tok), tok), :]
    angle = pos_col * freq_ref[...]
    cosine = jnp.cos(angle)
    lane = lax.broadcasted_iota(jnp.int32, (tok, 128), 1)
    first_half = (lane % ROPE) < (ROPE // 2)
    sine = jnp.where(first_half, -jnp.sin(angle), jnp.sin(angle))

    loads[0].wait()
    loads[1].wait()
    latent = ql[...]
    chunk = 512
    for start in range(0, nope_w, chunk):
        qrecv[0, :, start : start + chunk] = dot_nn(
            latent, wq[:, start : start + chunk]
        ).astype(BF16)
    loads[2].wait()
    rope_part = dot_nn(latent, wr[...])
    for start in range(0, rope_w, 128):
        part = rope_part[:, start : start + 128]
        swapped = jnp.where(
            first_half,
            pltpu.roll(part, 128 - ROPE // 2, 1),
            pltpu.roll(part, ROPE // 2, 1),
        )
        qrecv[0, :, nope_w + start : nope_w + start + 128] = (
            part * cosine + swapped * sine
        ).astype(BF16)

    small[2].wait()
    small[3].wait()
    counts = counts_ref[...]
    zero = jnp.zeros((1, tiles), jnp.int32)
    found = [zero, zero]
    index = [[zero] * LMAX, [zero] * LMAX]
    for slot in range(maxb):
        entry = lists_ref[slot : slot + 1, :]
        shard = entry % n_ctx
        local = entry // n_ctx
        valid = counts > slot
        for e in range(2):
            here = valid & (shard == me8 * 2 + e)
            for j in range(LMAX):
                index[e][j] = jnp.where(here & (found[e] == j), local + e * blocks, index[e][j])
            found[e] = found[e] + jnp.where(here, 1, 0)
    scal[...] = jnp.zeros_like(scal)
    for e in range(2):
        for j in range(LMAX):
            scal[e * LMAX + j : e * LMAX + j + 1, 0:tiles] = index[e][j]
        scal[2 * LMAX + e : 2 * LMAX + e + 1, 0:tiles] = found[e]
    scal_copy = pltpu.make_async_copy(scal, scal_smem, scal_sem)
    scal_copy.start()

    loads[3].wait()

    def double_key(b, carry):
        part = cache[core * blocks + b, :, LAT : LAT + ROPE]
        rope_key[core * blocks + b] = jnp.concatenate([part, part], axis=1)
        return carry

    lax.fori_loop(0, blocks, double_key, 0)

    scal_copy.wait()
    self_value = (1 - (core + lo) % 2) * (1 - (core + me_x) % 2)
    self_plane = 1 - (me_z + core) % 2
    pl.semaphore_wait(barrier, peers - 1 + 2 + peers - self_value + peers - self_plane)

    def remote(src, dst, send_sem, recv_sem, device):
        return pltpu.make_async_remote_copy(
            src_ref=src,
            dst_ref=dst,
            send_sem=send_sem,
            recv_sem=recv_sem,
            device_id=device,
            device_id_type=MESH,
        )

    def q_copy(held, pair, g, slot, send_sem):
        return remote(qrecv.at[held], qrecv.at[slot], send_sem, q_rs.at[slot], peer(pair, g))

    first_q = [q_copy(0, 0, 1, 1, q_ss.at[0])]
    relay_q = []
    last_q = []
    if n_y == 4:
        first_q += [q_copy(0, 1, g, mirror(1, g), q_ss.at[1 + g]) for g in range(2)]
        relay_q = [q_copy(1, 1, g, mirror(2, g), r_ss.at[g]) for g in range(2)]
        last_q = [
            q_copy(2 + me_x, 1, 1 - me_x, 6, r_ss.at[2]),
            q_copy(5 - me_x, 1, me_x, 7, r_ss.at[3]),
        ]
    for copy in first_q:
        copy.start()

    def exchange(which, src, dst, device):
        return remote(src, dst, ex_ss.at[which], ex_rs.at[which], device)

    def exchanges(side):
        half = pl.ds(side * blocks, blocks)
        own = pl.ds(core * blocks, blocks)
        return [
            exchange(0, cache_hbm, cache.at[half], sibling),
            exchange(1, rope_key.at[own], rope_key.at[half], sibling),
            exchange(2, wo_hbm, wo.at[0, side], sibling),
            exchange(3, wo_hbm, wo.at[1, core], across),
            exchange(4, wo.at[1, core], wo.at[1, side], sibling),
        ]

    swaps_out = exchanges(core)
    swaps_in = exchanges(1 - core)
    swaps_in[3] = swaps_out[3]
    for swap in swaps_out[:4]:
        swap.start()

    pairs = peers // 2
    seats = min(2, pairs)
    half_lane = lax.broadcasted_iota(jnp.int32, (1, 128), 1)
    half_mask = [
        (half_lane < ROPE).astype(F32).astype(BF16),
        (half_lane >= ROPE).astype(F32).astype(BF16),
    ]
    key_lane = lax.broadcasted_iota(jnp.int32, (1, keys), 1)
    key_slot = key_lane // BLK
    stat_lane = lax.broadcasted_iota(jnp.int32, (rows, 128), 1)
    scale = LOG2E * (NOPE + ROPE) ** (-0.5)

    loads[4].wait()

    def absorb(pair):
        group, first = 2, 2 * pair
        span = pl.ds(first, group)
        spot = pl.ds(pl.multiple_of(first * tok, tok), group * tok)
        for h in range(heads):
            nope = qrecv[span, :, h * NOPE : (h + 1) * NOPE].reshape(group * tok, NOPE)
            qabs[h, spot, 0:LAT] = dot_nn(nope, wk[h]).astype(BF16)
            start = nope_w + (h // 2) * 128
            pair = qrecv[span, :, start : start + 128].reshape(group * tok, 128)
            qabs[h, spot, LAT : LAT + 128] = pair * half_mask[h % 2]

    def attend(pair, part, seat):
        for g in range(2):
            slot = 2 * pair + g
            src = peer8(pair, g) * 2 + core
            stats = jnp.zeros((rows, 128), F32)
            for i in range(tiles_part):
                tile = src * tiles_src + part * tiles_part + i
                stage = (2 * seat + g) * tiles_part + i
                for j in range(2 * LMAX):
                    block = scal_smem[j, tile]
                    kstage[stage, j * BLK : (j + 1) * BLK, 0:LAT] = cache[block, :, 0:LAT]
                    kstage[stage, j * BLK : (j + 1) * BLK, LAT : LAT + 128] = rope_key[block]
                live_even = scal_smem[2 * LMAX, tile]
                live_odd = scal_smem[2 * LMAX + 1, tile]
                limit = jnp.where(key_slot < LMAX, live_even, live_odd + LMAX)
                bias = jnp.where(key_slot < limit, 0.0, NEG)
                start = pl.multiple_of(slot * tok + part * tok_part + i * TILE, TILE)
                query = qabs[:, pl.ds(start, TILE), :].reshape(rows, LAT + 128)
                score = dot_nt(query, kstage[stage]) * scale + bias
                peak = jnp.max(score, axis=1, keepdims=True)
                weight = jnp.exp2(score - peak)
                total = jnp.sum(weight, axis=1, keepdims=True)
                number = dot_nn(weight.astype(BF16), kstage[stage, :, 0:LAT])
                place = (2 * seat + g) * tok_part + i * TILE
                nabs[:, place : place + TILE, :] = number.astype(BF16).reshape(heads, TILE, LAT)
                stats = jnp.where(stat_lane == i, peak, stats)
                stats = jnp.where(stat_lane == tiles_part + i, total, stats)
            ssend[part, slot] = jnp.transpose(stats)[0 : 2 * tiles_part, :]

    def p_copy(part, pair, g, slot):
        held = 2 * pair + g
        return remote(
            psend.at[part, held], precv.at[part, slot],
            p_ss.at[part, held], p_rs.at[part, slot], peer(pair, g),
        )

    def s_copy(part, pair, g, slot):
        held = 2 * pair + g
        return remote(
            ssend.at[part, held], srecv.at[part, slot],
            s_ss.at[part, held], s_rs.at[part, slot], peer(pair, g),
        )

    def send_values(held):
        width = 2 * tok_part
        for h in range(heads):
            value = dot_nn(nabs[h, 0 : len(held) * width], wv[h]).astype(BF16)
            for seat, (pair, part) in enumerate(held):
                for g in range(2):
                    start = seat * width + g * tok_part
                    psend[part, 2 * pair + g, h] = value[start : start + tok_part, :]
        for pair, part in held:
            for g in range(2):

                @pl.when(2 * pair + g != 0)
                def _():
                    s_copy(part, pair, g, mirror(pair, g)).start()
                    p_copy(part, pair, g, mirror(pair, g)).start()

    def q_wait(slot):
        q_copy(0, 0, 1, slot, q_ss.at[0]).wait_recv()

    def attend_new(pair, carry):
        for g in range(2):

            @pl.when(2 * pair + g != 0)
            def _():
                q_wait(2 * pair + g)

        @pl.when(pair == 0)
        def _():
            for copy in relay_q:
                copy.start()

        if n_y == 4:

            @pl.when(pair == 1)
            def _():
                last_q[0].start()

            @pl.when(pair == 2)
            def _():
                last_q[1].start()

        absorb(pair)

        @pl.when(pair == 0)
        def _():
            loads[5].wait()
            swaps_in[0].wait_recv()
            swaps_in[1].wait_recv()

        for part in range(2):
            attend(pair, part, part)
        send_values([(pair, part) for part in range(2)])
        return carry

    def attend_again(part, seats):
        def step(n, carry):
            first = pairs - (n + 1) * seats
            held = [(first + seat, part) for seat in range(seats)]
            for seat, (pair, _) in enumerate(held):
                attend(pair, part, seat)
            send_values(held)
            return carry

        return step

    def combine(part):
        def p_wait(slot, carry):
            s_copy(part, 0, 0, slot).wait_recv()
            p_copy(part, 0, 0, slot).wait_recv()
            return carry

        lax.fori_loop(1, peers, p_wait, 0)
        srecv[part, 0] = ssend[part, 0]
        peaks = srecv[part, :, 0:tiles_part, :]
        sums = srecv[part, :, tiles_part : 2 * tiles_part, :]
        top = jnp.max(peaks, axis=0, keepdims=True)
        share = jnp.exp2(peaks - top)
        share = share / jnp.sum(share * sums, axis=0, keepdims=True)
        coef[...] = jnp.zeros_like(coef)
        for src in range(peers):
            coef[src * tiles_part : (src + 1) * tiles_part, :] = share[src]
        coef_t = jnp.transpose(coef[...])
        for i in range(tiles_part):
            mixed = jnp.zeros((rows, VDIM), F32)
            for src in range(peers):
                column = coef_t[:, src * tiles_part + i : src * tiles_part + i + 1]
                held = psend if src == 0 else precv
                term = held[part, src, :, i * TILE : (i + 1) * TILE, :].astype(F32)
                mixed = mixed + column * term.reshape(rows, VDIM)
            mixed = mixed.astype(BF16).reshape(heads, TILE, VDIM)
            for h in range(heads):
                vown[part, i * TILE : (i + 1) * TILE, h * VDIM : (h + 1) * VDIM] = mixed[h]

    def v_copy(part, n, slot):
        target = ((me_y + n // 2) % n_y) * 2 + (me_x + n) % 2
        return remote(
            vown.at[part], vall.at[part, slot // n_y, slot % n_y],
            v_ss.at[part, n], v_rs.at[part, slot],
            (me_z * 2 + core, target * 2 + me_x),
        )

    my_slot = lo * n_y + me_y

    def keeps(n):
        return (n == 0) & (core == lo) & (core == me_x)

    def gather(part):
        def v_start(n, carry):
            @pl.when(keeps(n))
            def _():
                vall[part, lo, me_y] = vown[part]

            @pl.when(jnp.logical_not(keeps(n)))
            def _():
                v_copy(part, n, my_slot).start()

            return carry

        lax.fori_loop(0, peers, v_start, 0)

    def o_copy(part, n, e, slot):
        plane = 2 * n + core
        return remote(
            osend.at[part, n, e], orecv.at[part, slot],
            o_ss.at[part, n, e], o_rs.at[part, slot],
            (plane * 2 + lo, me8 * 2 + e),
        )

    def stays(n, e):
        return (2 * n + core == me_z) & (core == e)

    def project(first, count):
        def v_wait(slot, carry):
            @pl.when((slot != my_slot) | (core != lo) | (core != me_x))
            def _():
                for part in range(first, first + count):
                    v_copy(part, 0, slot).wait_recv()

            return carry

        lax.fori_loop(0, peers, v_wait, 0)
        size = count * n_y * tok_part
        span = slice(first, first + count)
        for e in range(2):
            product = dot_nt(vall[span, lo].reshape(size, nope_w), wo[0, e])
            product = product + dot_nt(vall[span, 1 - lo].reshape(size, nope_w), wo[1, e])
            product = product.astype(BF16)
            for k in range(count):
                for n in range(n_y):
                    start = (k * n_y + n) * tok_part
                    osend[first + k, n, e] = product[start : start + tok_part, :]

        for part in range(first, first + count):

            def o_start(n, carry):
                at = (n + me_z // 2) % n_y
                for e in range(2):

                    @pl.when(stays(at, e))
                    def _():
                        orecv[part, me_z] = osend[part, at, e]

                    @pl.when(jnp.logical_not(stays(at, e)))
                    def _():
                        o_copy(part, at, e, me_z).start()

                return carry

            lax.fori_loop(0, n_y, o_start, 0)

    def collect(part):
        @pl.when(me_z % 2 != core)
        def _():
            o_copy(part, 0, 0, me_z).wait_recv()

        total = orecv[part, me_z].astype(F32)

        def add_plane(n, total):
            src = (me_z + n) % peers
            o_copy(part, 0, 0, src).wait_recv()
            return total + orecv[part, src].astype(F32)

        total = lax.fori_loop(1, peers, add_plane, total)
        out_ref[part * tok_part : (part + 1) * tok_part, :] = total.astype(BF16)

    lax.fori_loop(0, pairs, attend_new, 0)
    lax.fori_loop(0, 1, attend_again(2, pairs), 0)
    half = (pairs // seats + 1) // 2
    lax.fori_loop(0, half, attend_again(3, seats), 0)
    for part in range(2):
        combine(part)
        gather(part)
    lax.fori_loop(half, pairs // seats, attend_again(3, seats), 0)
    combine(2)
    gather(2)
    loads[6].wait()
    swaps_in[2].wait_recv()
    swaps_in[3].wait_recv()
    swaps_out[4].start()
    swaps_in[4].wait_recv()
    project(0, 2)
    combine(3)
    gather(3)
    project(2, 1)
    project(3, 1)
    for part in range(parts):
        collect(part)

    for swap in swaps_out:
        swap.wait_send()

    for copy in first_q + relay_q + last_q:
        copy.wait_send()

    def drain_peers(pair, carry):
        for g in range(2):

            @pl.when(2 * pair + g != 0)
            def _():
                for part in range(parts):
                    p_copy(part, pair, g, 0).wait_send()
                    s_copy(part, pair, g, 0).wait_send()

        return carry

    lax.fori_loop(0, pairs, drain_peers, 0)

    def drain_values(n, carry):
        @pl.when(jnp.logical_not(keeps(n)))
        def _():
            for part in range(parts):
                v_copy(part, n, my_slot).wait_send()

        return carry

    lax.fori_loop(0, peers, drain_values, 0)

    def drain_planes(n, carry):
        for e in range(2):

            @pl.when(jnp.logical_not(stays(n, e)))
            def _():
                for part in range(parts):
                    o_copy(part, n, e, me_z).wait_send()

        return carry

    lax.fori_loop(0, n_y, drain_planes, 0)


def local(
    n_ctx, n_head,
    query_latent, w_query_nope, w_query_rope, w_absorb_key, w_absorb_value, w_output,
    latent_cache, block_lists, block_counts, positions,
):
    tok, q_lat = query_latent.shape
    heads = w_absorb_key.shape[0]
    blocks = latent_cache.shape[0]
    tiles, maxb = block_lists.shape
    cols = w_output.shape[1]
    peers = n_ctx // 2
    tiles_src = tok // TILE
    nope_w = heads * NOPE
    rope_w = heads * ROPE
    rows = heads * TILE
    keys = 2 * LMAX * BLK
    half = ROPE // 2
    frequency = 10000.0 ** (-2.0 * np.arange(half, dtype=np.float64) / ROPE)
    frequency = np.tile(frequency.astype(np.float32), 128 // half)[None, :]
    parts = PARTS
    n_y = peers // 2
    tok_part = tok // parts
    sizes = (n_ctx, n_head, heads, tok, blocks, maxb, tiles, parts)
    hbm = pl.BlockSpec(memory_space=pltpu.HBM)
    vmem = pl.BlockSpec(memory_space=pltpu.VMEM)
    dma = pltpu.SemaphoreType.DMA
    return pl.pallas_call(
        functools.partial(kernel, sizes),
        out_shape=jax.ShapeDtypeStruct((tok, cols), BF16),
        in_specs=[hbm] * 11,
        out_specs=vmem,
        scratch_shapes=[
            pltpu.VMEM((tok, q_lat), BF16),
            pltpu.VMEM((q_lat, nope_w), BF16),
            pltpu.VMEM((q_lat, rope_w), BF16),
            pltpu.VMEM((heads, NOPE, LAT), BF16),
            pltpu.VMEM((heads, LAT, VDIM), BF16),
            pltpu.VMEM((2, 2, cols, heads * VDIM), BF16),
            pltpu.VMEM((2 * blocks, BLK, LAT + ROPE), BF16),
            pltpu.VMEM((2 * blocks, BLK, 128), BF16),
            pltpu.VMEM((maxb, tiles), jnp.int32),
            pltpu.VMEM((1, tiles), jnp.int32),
            pltpu.VMEM((positions.shape[0] // 128, 128), jnp.int32),
            pltpu.VMEM((1, 128), F32),
            pltpu.VMEM((16, 128), jnp.int32),
            pltpu.SMEM((16, 128), jnp.int32),
            pltpu.VMEM((128, 128), F32),
            pltpu.VMEM((peers, tok, nope_w + rope_w), BF16),
            pltpu.VMEM((heads, peers * tok, LAT + 128), BF16),
            pltpu.VMEM((max(4, peers) * tiles_src // parts, keys, LAT + 128), BF16),
            pltpu.VMEM((heads, max(4, peers) * tok_part, LAT), BF16),
            pltpu.VMEM((parts, peers, heads, tok_part, VDIM), BF16),
            pltpu.VMEM((parts, peers, heads, tok_part, VDIM), BF16),
            pltpu.VMEM((parts, peers, 2 * tiles_src // parts, 128), F32),
            pltpu.VMEM((parts, peers, 2 * tiles_src // parts, 128), F32),
            pltpu.VMEM((128, 128), F32),
            pltpu.VMEM((parts, tok_part, nope_w), BF16),
            pltpu.VMEM((parts, 2, n_y, tok_part, nope_w), BF16),
            pltpu.VMEM((parts, n_y, 2, tok_part, cols), BF16),
            pltpu.VMEM((parts, peers, tok_part, cols), BF16),
            dma((11,)),
            dma((5,)),
            dma((5,)),
            dma(()),
            dma((3,)),
            dma((peers,)),
            dma((4,)),
            dma((parts, peers)),
            dma((parts, peers)),
            dma((parts, peers)),
            dma((parts, peers)),
            dma((parts, peers)),
            dma((parts, peers)),
            dma((parts, n_y, 2)),
            dma((parts, peers)),
        ],
        compiler_params=pltpu.CompilerParams(
            collective_id=0, has_side_effects=True, vmem_limit_bytes=63 * 1024 * 1024
        ),
    )(
        query_latent, w_query_nope, w_query_rope, w_absorb_key, w_absorb_value, w_output.T,
        latent_cache, block_lists.T, block_counts.reshape(1, tiles),
        positions.reshape(positions.shape[0] // 128, 128), jnp.asarray(frequency),
    )


def solution(mesh):
    in_specs = (
        P("ctx", None),
        P(None, "head"),
        P(None, "head"),
        P("head", None, None),
        P("head", None, None),
        P("head", "ctx"),
        P(None, "ctx", None),
        P(),
        P(),
        P(),
    )
    run = functools.partial(local, mesh.shape["ctx"], mesh.shape["head"])
    return jax.shard_map(
        run, mesh=mesh, in_specs=in_specs, out_specs=P("head", "ctx"), check_vma=False
    )
```

```python
import functools

import jax
import jax.numpy as jnp
import numpy as np
from jax import lax
from jax.experimental import pallas as pl
from jax.experimental.pallas import tpu as pltpu
from jax.sharding import PartitionSpec as P

LAT = 512
ROPE = 64
NOPE = 128
VDIM = 128
BLK = 64
TILE = 16
LMAX = 4
NEG = -1e30
PARTS = 4
LOG2E = 1.4426950408889634
MESH = pl.DeviceIdType.MESH
F32 = jnp.float32
BF16 = jnp.bfloat16


def dot_nt(a, b):
    return lax.dot_general(a, b, (((1,), (1,)), ((), ())), preferred_element_type=F32)


def dot_nn(a, b):
    return jnp.dot(a, b, preferred_element_type=F32)


def kernel(
    sizes,
    ql_hbm, wq_hbm, wr_hbm, wk_hbm, wv_hbm, wo_hbm, cache_hbm,
    lists_hbm, counts_hbm, pos_hbm, freq_hbm,
    out_ref,
    ql, wq, wr, wk, wv, wo, cache, rope_key,
    lists_ref, counts_ref, pos_ref, freq_ref, scal, scal_smem, posbuf,
    qrecv, qabs, kstage, nabs,
    psend, precv, ssend, srecv, coef, vown, vall, osend, orecv,
    in_sem, ex_ss, ex_rs, scal_sem,
    q_ss, q_rs, r_ss, p_ss, p_rs, s_ss, s_rs, v_ss, v_rs, o_ss, o_rs,
):
    n_ctx, n_head, heads, tok, blocks, maxb, tiles, parts = sizes
    peers = n_ctx // 2
    n_y = peers // 2
    me_h = lax.axis_index("head")
    me_c = lax.axis_index("ctx")
    me8 = me_c // 2
    core = me_c % 2
    me_y = me8 // 2
    me_x = me8 % 2
    me_z = me_h // 2
    lo = me_h % 2
    sibling = (me_h, me8 * 2 + (1 - core))
    across = (me_z * 2 + (1 - lo), me_c)
    nope_w = heads * NOPE
    rope_w = heads * ROPE
    tiles_src = tok // TILE
    tiles_part = tiles_src // parts
    tok_part = tok // parts
    rows = heads * TILE
    keys = 2 * LMAX * BLK

    def shift_of(pair, g):
        middle = ((pair + 1) // 2) % 2
        dx = middle * (pair // 2) + (1 - middle) * g
        dy = middle * (3 - 2 * g) + (1 - middle) * 2 * (pair // 3)
        return dy, dx

    def peer8(pair, g):
        dy, dx = shift_of(pair, g)
        return ((me_y + dy) % n_y) * 2 + (me_x + dx) % 2

    def peer(pair, g):
        return (me_h, peer8(pair, g) * 2 + core)

    def mirror(pair, g):
        middle = ((pair + 1) // 2) % 2
        return 2 * pair + middle * (1 - g) + (1 - middle) * g

    small = [
        pltpu.make_async_copy(pos_hbm, pos_ref, in_sem.at[7]),
        pltpu.make_async_copy(freq_hbm, freq_ref, in_sem.at[8]),
        pltpu.make_async_copy(lists_hbm, lists_ref, in_sem.at[9]),
        pltpu.make_async_copy(counts_hbm, counts_ref, in_sem.at[10]),
    ]
    loads = [
        pltpu.make_async_copy(ql_hbm, ql, in_sem.at[0]),
        pltpu.make_async_copy(wq_hbm, wq, in_sem.at[1]),
        pltpu.make_async_copy(wr_hbm, wr, in_sem.at[2]),
        pltpu.make_async_copy(
            cache_hbm, cache.at[pl.ds(core * blocks, blocks)], in_sem.at[3]
        ),
        pltpu.make_async_copy(wk_hbm, wk, in_sem.at[4]),
        pltpu.make_async_copy(wv_hbm, wv, in_sem.at[5]),
        pltpu.make_async_copy(wo_hbm, wo.at[0, core], in_sem.at[6]),
    ]
    for load in small + loads:
        load.start()

    barrier = pltpu.get_barrier_semaphore()

    def greet(device):
        pl.semaphore_signal(barrier, inc=1, device_id=device, device_id_type=MESH)

    def greet_peers(pair, carry):
        for g in range(2):

            @pl.when(2 * pair + g != 0)
            def _():
                greet(peer(pair, g))

        return carry

    def value_source(n, other):
        return (me_z * 2 + other, (n * 2 + core) * 2 + lo)

    def greet_value_sources(n, carry):
        for other in range(2):

            @pl.when((n != me_y) | (other != lo) | (core != me_x) | (lo != core))
            def _():
                greet(value_source(n, other))

        return carry

    def greet_planes(n, carry):
        @pl.when((n != me_z) | (me_z % 2 != core))
        def _():
            greet((n * 2 + lo, me8 * 2 + me_z % 2))

        return carry

    greet(sibling)
    greet(across)
    lax.fori_loop(0, peers // 2, greet_peers, 0)
    lax.fori_loop(0, n_y, greet_value_sources, 0)
    lax.fori_loop(0, peers, greet_planes, 0)

    small[0].wait()
    small[1].wait()
    pos_row = pos_ref[pl.ds(me8, 1), :].astype(F32)
    posbuf[...] = jnp.transpose(jnp.broadcast_to(pos_row, (128, 128)))
    pos_col = posbuf[pl.ds(pl.multiple_of(core * tok, tok), tok), :]
    angle = pos_col * freq_ref[...]
    cosine = jnp.cos(angle)
    lane = lax.broadcasted_iota(jnp.int32, (tok, 128), 1)
    first_half = (lane % ROPE) < (ROPE // 2)
    sine = jnp.where(first_half, -jnp.sin(angle), jnp.sin(angle))

    loads[0].wait()
    loads[1].wait()
    latent = ql[...]
    chunk = 512
    for start in range(0, nope_w, chunk):
        qrecv[0, :, start : start + chunk] = dot_nn(
            latent, wq[:, start : start + chunk]
        ).astype(BF16)
    loads[2].wait()
    rope_part = dot_nn(latent, wr[...])
    for start in range(0, rope_w, 128):
        part = rope_part[:, start : start + 128]
        swapped = jnp.where(
            first_half,
            pltpu.roll(part, 128 - ROPE // 2, 1),
            pltpu.roll(part, ROPE // 2, 1),
        )
        qrecv[0, :, nope_w + start : nope_w + start + 128] = (
            part * cosine + swapped * sine
        ).astype(BF16)

    small[2].wait()
    small[3].wait()
    counts = counts_ref[...]
    zero = jnp.zeros((1, tiles), jnp.int32)
    found = [zero, zero]
    index = [[zero] * LMAX, [zero] * LMAX]
    for slot in range(maxb):
        entry = lists_ref[slot : slot + 1, :]
        shard = entry % n_ctx
        local = entry // n_ctx
        valid = counts > slot
        for e in range(2):
            here = valid & (shard == me8 * 2 + e)
            for j in range(LMAX):
                index[e][j] = jnp.where(here & (found[e] == j), local + e * blocks, index[e][j])
            found[e] = found[e] + jnp.where(here, 1, 0)
    scal[...] = jnp.zeros_like(scal)
    for e in range(2):
        for j in range(LMAX):
            scal[e * LMAX + j : e * LMAX + j + 1, 0:tiles] = index[e][j]
        scal[2 * LMAX + e : 2 * LMAX + e + 1, 0:tiles] = found[e]
    scal_copy = pltpu.make_async_copy(scal, scal_smem, scal_sem)
    scal_copy.start()

    loads[3].wait()

    def double_key(b, carry):
        part = cache[core * blocks + b, :, LAT : LAT + ROPE]
        rope_key[core * blocks + b] = jnp.concatenate([part, part], axis=1)
        return carry

    lax.fori_loop(0, blocks, double_key, 0)

    scal_copy.wait()
    self_value = (1 - (core + lo) % 2) * (1 - (core + me_x) % 2)
    self_plane = 1 - (me_z + core) % 2
    pl.semaphore_wait(barrier, peers - 1 + 2 + peers - self_value + peers - self_plane)

    def remote(src, dst, send_sem, recv_sem, device):
        return pltpu.make_async_remote_copy(
            src_ref=src,
            dst_ref=dst,
            send_sem=send_sem,
            recv_sem=recv_sem,
            device_id=device,
            device_id_type=MESH,
        )

    def q_copy(held, pair, g, slot, send_sem):
        return remote(qrecv.at[held], qrecv.at[slot], send_sem, q_rs.at[slot], peer(pair, g))

    first_q = [q_copy(0, 0, 1, 1, q_ss.at[0])]
    relay_q = []
    last_q = []
    if n_y == 4:
        first_q += [q_copy(0, 1, g, mirror(1, g), q_ss.at[1 + g]) for g in range(2)]
        relay_q = [q_copy(1, 1, g, mirror(2, g), r_ss.at[g]) for g in range(2)]
        last_q = [
            q_copy(2 + me_x, 1, 1 - me_x, 6, r_ss.at[2]),
            q_copy(5 - me_x, 1, me_x, 7, r_ss.at[3]),
        ]
    for copy in first_q:
        copy.start()

    def exchange(which, src, dst, device):
        return remote(src, dst, ex_ss.at[which], ex_rs.at[which], device)

    def exchanges(side):
        half = pl.ds(side * blocks, blocks)
        own = pl.ds(core * blocks, blocks)
        return [
            exchange(0, cache_hbm, cache.at[half], sibling),
            exchange(1, rope_key.at[own], rope_key.at[half], sibling),
            exchange(2, wo_hbm, wo.at[0, side], sibling),
            exchange(3, wo_hbm, wo.at[1, core], across),
            exchange(4, wo.at[1, core], wo.at[1, side], sibling),
        ]

    swaps_out = exchanges(core)
    swaps_in = exchanges(1 - core)
    swaps_in[3] = swaps_out[3]
    for swap in swaps_out[:4]:
        swap.start()

    pairs = peers // 2
    seats = min(2, pairs)
    half_lane = lax.broadcasted_iota(jnp.int32, (1, 128), 1)
    half_mask = [
        (half_lane < ROPE).astype(F32).astype(BF16),
        (half_lane >= ROPE).astype(F32).astype(BF16),
    ]
    key_lane = lax.broadcasted_iota(jnp.int32, (1, keys), 1)
    key_slot = key_lane // BLK
    stat_lane = lax.broadcasted_iota(jnp.int32, (rows, 128), 1)
    scale = LOG2E * (NOPE + ROPE) ** (-0.5)

    loads[4].wait()

    def absorb(pair):
        group, first = 2, 2 * pair
        span = pl.ds(first, group)
        spot = pl.ds(pl.multiple_of(first * tok, tok), group * tok)
        for h in range(heads):
            nope = qrecv[span, :, h * NOPE : (h + 1) * NOPE].reshape(group * tok, NOPE)
            qabs[h, spot, 0:LAT] = dot_nn(nope, wk[h]).astype(BF16)
            start = nope_w + (h // 2) * 128
            pair = qrecv[span, :, start : start + 128].reshape(group * tok, 128)
            qabs[h, spot, LAT : LAT + 128] = pair * half_mask[h % 2]

    def attend(pair, part, seat):
        for g in range(2):
            slot = 2 * pair + g
            src = peer8(pair, g) * 2 + core
            stats = jnp.zeros((rows, 128), F32)
            for i in range(tiles_part):
                tile = src * tiles_src + part * tiles_part + i
                stage = (2 * seat + g) * tiles_part + i
                for j in range(2 * LMAX):
                    block = scal_smem[j, tile]
                    kstage[stage, j * BLK : (j + 1) * BLK, 0:LAT] = cache[block, :, 0:LAT]
                    kstage[stage, j * BLK : (j + 1) * BLK, LAT : LAT + 128] = rope_key[block]
                live_even = scal_smem[2 * LMAX, tile]
                live_odd = scal_smem[2 * LMAX + 1, tile]
                limit = jnp.where(key_slot < LMAX, live_even, live_odd + LMAX)
                bias = jnp.where(key_slot < limit, 0.0, NEG)
                start = pl.multiple_of(slot * tok + part * tok_part + i * TILE, TILE)
                query = qabs[:, pl.ds(start, TILE), :].reshape(rows, LAT + 128)
                score = dot_nt(query, kstage[stage]) * scale + bias
                peak = jnp.max(score, axis=1, keepdims=True)
                weight = jnp.exp2(score - peak)
                total = jnp.sum(weight, axis=1, keepdims=True)
                number = dot_nn(weight.astype(BF16), kstage[stage, :, 0:LAT])
                place = (2 * seat + g) * tok_part + i * TILE
                nabs[:, place : place + TILE, :] = number.astype(BF16).reshape(heads, TILE, LAT)
                stats = jnp.where(stat_lane == i, peak, stats)
                stats = jnp.where(stat_lane == tiles_part + i, total, stats)
            ssend[part, slot] = jnp.transpose(stats)[0 : 2 * tiles_part, :]

    def p_copy(part, pair, g, slot):
        held = 2 * pair + g
        return remote(
            psend.at[part, held], precv.at[part, slot],
            p_ss.at[part, held], p_rs.at[part, slot], peer(pair, g),
        )

    def s_copy(part, pair, g, slot):
        held = 2 * pair + g
        return remote(
            ssend.at[part, held], srecv.at[part, slot],
            s_ss.at[part, held], s_rs.at[part, slot], peer(pair, g),
        )

    def send_values(held):
        width = 2 * tok_part
        for h in range(heads):
            value = dot_nn(nabs[h, 0 : len(held) * width], wv[h]).astype(BF16)
            for seat, (pair, part) in enumerate(held):
                for g in range(2):
                    start = seat * width + g * tok_part
                    psend[part, 2 * pair + g, h] = value[start : start + tok_part, :]
        for pair, part in held:
            for g in range(2):

                @pl.when(2 * pair + g != 0)
                def _():
                    s_copy(part, pair, g, mirror(pair, g)).start()
                    p_copy(part, pair, g, mirror(pair, g)).start()

    def q_wait(slot):
        q_copy(0, 0, 1, slot, q_ss.at[0]).wait_recv()

    def attend_new(pair, carry):
        for g in range(2):

            @pl.when(2 * pair + g != 0)
            def _():
                q_wait(2 * pair + g)

        @pl.when(pair == 0)
        def _():
            for copy in relay_q:
                copy.start()

        if n_y == 4:

            @pl.when(pair == 1)
            def _():
                last_q[0].start()

            @pl.when(pair == 2)
            def _():
                last_q[1].start()

        absorb(pair)

        @pl.when(pair == 0)
        def _():
            loads[5].wait()
            swaps_in[0].wait_recv()
            swaps_in[1].wait_recv()

        for part in range(2):
            attend(pair, part, part)
        send_values([(pair, part) for part in range(2)])
        return carry

    def attend_again(part, seats):
        def step(n, carry):
            first = pairs - (n + 1) * seats
            held = [(first + seat, part) for seat in range(seats)]
            for seat, (pair, _) in enumerate(held):
                attend(pair, part, seat)
            send_values(held)
            return carry

        return step

    def combine(part):
        def p_wait(slot, carry):
            s_copy(part, 0, 0, slot).wait_recv()
            p_copy(part, 0, 0, slot).wait_recv()
            return carry

        lax.fori_loop(1, peers, p_wait, 0)
        srecv[part, 0] = ssend[part, 0]
        peaks = srecv[part, :, 0:tiles_part, :]
        sums = srecv[part, :, tiles_part : 2 * tiles_part, :]
        top = jnp.max(peaks, axis=0, keepdims=True)
        share = jnp.exp2(peaks - top)
        share = share / jnp.sum(share * sums, axis=0, keepdims=True)
        coef[...] = jnp.zeros_like(coef)
        for src in range(peers):
            coef[src * tiles_part : (src + 1) * tiles_part, :] = share[src]
        coef_t = jnp.transpose(coef[...])
        for i in range(tiles_part):
            mixed = jnp.zeros((rows, VDIM), F32)
            for src in range(peers):
                column = coef_t[:, src * tiles_part + i : src * tiles_part + i + 1]
                held = psend if src == 0 else precv
                term = held[part, src, :, i * TILE : (i + 1) * TILE, :].astype(F32)
                mixed = mixed + column * term.reshape(rows, VDIM)
            mixed = mixed.astype(BF16).reshape(heads, TILE, VDIM)
            for h in range(heads):
                vown[part, i * TILE : (i + 1) * TILE, h * VDIM : (h + 1) * VDIM] = mixed[h]

    def v_copy(part, n, slot):
        target = ((me_y + n // 2) % n_y) * 2 + (me_x + n) % 2
        return remote(
            vown.at[part], vall.at[part, slot // n_y, slot % n_y],
            v_ss.at[part, n], v_rs.at[part, slot],
            (me_z * 2 + core, target * 2 + me_x),
        )

    my_slot = lo * n_y + me_y

    def keeps(n):
        return (n == 0) & (core == lo) & (core == me_x)

    def gather(part):
        def v_start(step, carry):
            n = (step + peers // 2) % peers

            @pl.when(keeps(n))
            def _():
                vall[part, lo, me_y] = vown[part]

            @pl.when(jnp.logical_not(keeps(n)))
            def _():
                v_copy(part, n, my_slot).start()

            return carry

        lax.fori_loop(0, peers, v_start, 0)

    def o_copy(part, n, e, slot):
        plane = 2 * n + core
        return remote(
            osend.at[part, n, e], orecv.at[part, slot],
            o_ss.at[part, n, e], o_rs.at[part, slot],
            (plane * 2 + lo, me8 * 2 + e),
        )

    def stays(n, e):
        return (2 * n + core == me_z) & (core == e)

    def project(first, count):
        def v_wait(slot, carry):
            @pl.when((slot != my_slot) | (core != lo) | (core != me_x))
            def _():
                for part in range(first, first + count):
                    v_copy(part, 0, slot).wait_recv()

            return carry

        lax.fori_loop(0, peers, v_wait, 0)
        size = count * n_y * tok_part
        span = slice(first, first + count)
        for e in range(2):
            product = dot_nt(vall[span, lo].reshape(size, nope_w), wo[0, e])
            product = product + dot_nt(vall[span, 1 - lo].reshape(size, nope_w), wo[1, e])
            product = product.astype(BF16)
            for k in range(count):
                for n in range(n_y):
                    start = (k * n_y + n) * tok_part
                    osend[first + k, n, e] = product[start : start + tok_part, :]

        for part in range(first, first + count):

            def o_start(n, carry):
                at = (n + me_z // 2 + n_y // 2) % n_y
                for e in range(2):

                    @pl.when(stays(at, e))
                    def _():
                        orecv[part, me_z] = osend[part, at, e]

                    @pl.when(jnp.logical_not(stays(at, e)))
                    def _():
                        o_copy(part, at, e, me_z).start()

                return carry

            lax.fori_loop(0, n_y, o_start, 0)

    def collect(part):
        @pl.when(me_z % 2 != core)
        def _():
            o_copy(part, 0, 0, me_z).wait_recv()

        total = orecv[part, me_z].astype(F32)

        def add_plane(n, total):
            src = (me_z + n) % peers
            o_copy(part, 0, 0, src).wait_recv()
            return total + orecv[part, src].astype(F32)

        total = lax.fori_loop(1, peers, add_plane, total)
        out_ref[part * tok_part : (part + 1) * tok_part, :] = total.astype(BF16)

    lax.fori_loop(0, pairs, attend_new, 0)
    lax.fori_loop(0, 1, attend_again(2, pairs), 0)
    half = (pairs // seats + 1) // 2
    lax.fori_loop(0, half, attend_again(3, seats), 0)
    for part in range(2):
        combine(part)
        gather(part)
    lax.fori_loop(half, pairs // seats, attend_again(3, seats), 0)
    combine(2)
    gather(2)
    loads[6].wait()
    swaps_in[2].wait_recv()
    swaps_in[3].wait_recv()
    swaps_out[4].start()
    swaps_in[4].wait_recv()
    project(0, 2)
    combine(3)
    gather(3)
    project(2, 1)
    project(3, 1)
    for part in range(parts):
        collect(part)

    for swap in swaps_out:
        swap.wait_send()

    for copy in first_q + relay_q + last_q:
        copy.wait_send()

    def drain_peers(pair, carry):
        for g in range(2):

            @pl.when(2 * pair + g != 0)
            def _():
                for part in range(parts):
                    p_copy(part, pair, g, 0).wait_send()
                    s_copy(part, pair, g, 0).wait_send()

        return carry

    lax.fori_loop(0, pairs, drain_peers, 0)

    def drain_values(n, carry):
        @pl.when(jnp.logical_not(keeps(n)))
        def _():
            for part in range(parts):
                v_copy(part, n, my_slot).wait_send()

        return carry

    lax.fori_loop(0, peers, drain_values, 0)

    def drain_planes(n, carry):
        for e in range(2):

            @pl.when(jnp.logical_not(stays(n, e)))
            def _():
                for part in range(parts):
                    o_copy(part, n, e, me_z).wait_send()

        return carry

    lax.fori_loop(0, n_y, drain_planes, 0)


def local(
    n_ctx, n_head,
    query_latent, w_query_nope, w_query_rope, w_absorb_key, w_absorb_value, w_output,
    latent_cache, block_lists, block_counts, positions,
):
    tok, q_lat = query_latent.shape
    heads = w_absorb_key.shape[0]
    blocks = latent_cache.shape[0]
    tiles, maxb = block_lists.shape
    cols = w_output.shape[1]
    peers = n_ctx // 2
    tiles_src = tok // TILE
    nope_w = heads * NOPE
    rope_w = heads * ROPE
    rows = heads * TILE
    keys = 2 * LMAX * BLK
    half = ROPE // 2
    frequency = 10000.0 ** (-2.0 * np.arange(half, dtype=np.float64) / ROPE)
    frequency = np.tile(frequency.astype(np.float32), 128 // half)[None, :]
    parts = PARTS
    n_y = peers // 2
    tok_part = tok // parts
    sizes = (n_ctx, n_head, heads, tok, blocks, maxb, tiles, parts)
    hbm = pl.BlockSpec(memory_space=pltpu.HBM)
    vmem = pl.BlockSpec(memory_space=pltpu.VMEM)
    dma = pltpu.SemaphoreType.DMA
    return pl.pallas_call(
        functools.partial(kernel, sizes),
        out_shape=jax.ShapeDtypeStruct((tok, cols), BF16),
        in_specs=[hbm] * 11,
        out_specs=vmem,
        scratch_shapes=[
            pltpu.VMEM((tok, q_lat), BF16),
            pltpu.VMEM((q_lat, nope_w), BF16),
            pltpu.VMEM((q_lat, rope_w), BF16),
            pltpu.VMEM((heads, NOPE, LAT), BF16),
            pltpu.VMEM((heads, LAT, VDIM), BF16),
            pltpu.VMEM((2, 2, cols, heads * VDIM), BF16),
            pltpu.VMEM((2 * blocks, BLK, LAT + ROPE), BF16),
            pltpu.VMEM((2 * blocks, BLK, 128), BF16),
            pltpu.VMEM((maxb, tiles), jnp.int32),
            pltpu.VMEM((1, tiles), jnp.int32),
            pltpu.VMEM((positions.shape[0] // 128, 128), jnp.int32),
            pltpu.VMEM((1, 128), F32),
            pltpu.VMEM((16, 128), jnp.int32),
            pltpu.SMEM((16, 128), jnp.int32),
            pltpu.VMEM((128, 128), F32),
            pltpu.VMEM((peers, tok, nope_w + rope_w), BF16),
            pltpu.VMEM((heads, peers * tok, LAT + 128), BF16),
            pltpu.VMEM((max(4, peers) * tiles_src // parts, keys, LAT + 128), BF16),
            pltpu.VMEM((heads, max(4, peers) * tok_part, LAT), BF16),
            pltpu.VMEM((parts, peers, heads, tok_part, VDIM), BF16),
            pltpu.VMEM((parts, peers, heads, tok_part, VDIM), BF16),
            pltpu.VMEM((parts, peers, 2 * tiles_src // parts, 128), F32),
            pltpu.VMEM((parts, peers, 2 * tiles_src // parts, 128), F32),
            pltpu.VMEM((128, 128), F32),
            pltpu.VMEM((parts, tok_part, nope_w), BF16),
            pltpu.VMEM((parts, 2, n_y, tok_part, nope_w), BF16),
            pltpu.VMEM((parts, n_y, 2, tok_part, cols), BF16),
            pltpu.VMEM((parts, peers, tok_part, cols), BF16),
            dma((11,)),
            dma((5,)),
            dma((5,)),
            dma(()),
            dma((3,)),
            dma((peers,)),
            dma((4,)),
            dma((parts, peers)),
            dma((parts, peers)),
            dma((parts, peers)),
            dma((parts, peers)),
            dma((parts, peers)),
            dma((parts, peers)),
            dma((parts, n_y, 2)),
            dma((parts, peers)),
        ],
        compiler_params=pltpu.CompilerParams(
            collective_id=0, has_side_effects=True, vmem_limit_bytes=63 * 1024 * 1024
        ),
    )(
        query_latent, w_query_nope, w_query_rope, w_absorb_key, w_absorb_value, w_output.T,
        latent_cache, block_lists.T, block_counts.reshape(1, tiles),
        positions.reshape(positions.shape[0] // 128, 128), jnp.asarray(frequency),
    )


def solution(mesh):
    in_specs = (
        P("ctx", None),
        P(None, "head"),
        P(None, "head"),
        P("head", None, None),
        P("head", None, None),
        P("head", "ctx"),
        P(None, "ctx", None),
        P(),
        P(),
        P(),
    )
    run = functools.partial(local, mesh.shape["ctx"], mesh.shape["head"])
    return jax.shard_map(
        run, mesh=mesh, in_specs=in_specs, out_specs=P("head", "ctx"), check_vma=False
    )
```
